256 devices in a mesh: row: 16 (over y_lo, x, core), col: 16 (over y_hi, z).
Axes of the slice: x: 4, y: 4 (y_hi: 2, y_lo: 2; y = y_hi * 2 + y_lo), z: 8, core: 2. Of those that a mesh axis runs over, the one named last changes fastest.
Arguments:
- places: float32 [256, 4, 256], P(('row', 'col')), may hold values from 0 to 8, as said below
- omega: bfloat16 [256, 64, 256], P(('row', 'col')), may hold values from -6 to 6
- pairs: int32 [32768, 2], P(('row', 'col')), may hold values from -1 to 255, as said below
Outputs:
- bases: float32 [256, 64, 256], P(('row', 'col'))
- coeffs: bfloat16 [32768, 64, 256], P(('row', 'col'))
The draws below stay inside these ranges and needn't reach their ends.
Inputs may be any that keep to these rules, and one draw needn't show every extreme that they name: Device d (in row+col order, grid row d // 16 = a, grid column d % 16 = b) holds slots d * 128 to (d + 1) * 128 - 1. Its live slots come first and hold distinct pairs (t, s) with t % 16 = b and s // (1 * 16) = a; the rest hold -1 in both columns. Every block is the target of a live slot on each device whose target set contains it. Each device has at least 32 and at most 128 live slots, and some device has all 128. `places`: rows 0 to 2 are coordinates, row 3 holds weights of 0.25 or more.
All inputs are finite; a program needn't handle non-finite values.
Results may differ from the reference program's by a relative error of at most 0.0027.
The reference program's roundings to bfloat16 on the way (of `kernel` and `basis_b`) count: a program that leaves them out, or rounds other values in their place, can miss the bound.
Values may be sent and summed in bfloat16 or wider, within the bound.
A program may use at most 64 MiB of HBM per device.

```python
import math
import jax
import jax.numpy as jnp
from jax import lax

BLK = 256
RANK = 64
BPD = 1
NB = 256
TSET = 16
SSET = 16
PAIR_SLOTS_LIMIT = 128
NPAIRS = 32768


def draw_places(key, part):
    coord_key = jax.random.fold_in(key, 11)
    weight_key = jax.random.fold_in(key, 12)
    jitter_key = jax.random.fold_in(key, 13)
    radius_key = jax.random.fold_in(key, 14)
    side = int(NB ** (1.0 / 3.0) + 0.999)
    spacing = 8.0 / side
    index = jnp.arange(NB, dtype=jnp.int32)
    cells = jnp.stack([index % side, index // side % side, index // (side * side) % side], axis=1).astype(jnp.float32)
    jitter = jax.random.uniform(jitter_key, (NB, 3), jnp.float32, -0.1, 0.1) * spacing
    centres = (cells + 0.5) * spacing + jitter
    direction = jax.random.normal(coord_key, (NB, 3, BLK), jnp.float32)
    length = jnp.sqrt(jnp.sum(direction * direction, axis=1, keepdims=True) + 1e-06)
    radius = jax.random.uniform(radius_key, (NB, 1, 1), jnp.float32, 0.22, 0.3) * spacing
    weights = jnp.exp(jax.random.uniform(weight_key, (NB, 1, BLK), jnp.float32, jnp.log(0.5), jnp.log(2.0)))
    coords = centres[:, :, None] + radius * direction / length
    coords = jnp.clip(coords, 0.0, 8.0)
    return jnp.concatenate([coords, weights], axis=1).astype(jnp.float32)


def draw_pairs(key, part):
    device_count = NPAIRS // PAIR_SLOTS_LIMIT
    col_count = SSET // BPD
    pair_combinations = TSET * SSET
    full_device = jax.random.randint(jax.random.fold_in(key, 21), (), 0, device_count)

    def per_device(device):
        sub_key = jax.random.fold_in(key, device)
        rank_values = jax.random.permutation(jax.random.fold_in(sub_key, 1), pair_combinations).astype(jnp.int32)
        forced_src = jax.random.randint(jax.random.fold_in(sub_key, 2), (TSET,), 0, SSET)
        required_sources = jnp.arange(TSET, dtype=jnp.int32) * SSET + forced_src
        extra_credit = jnp.zeros((pair_combinations,), jnp.int32).at[required_sources].set(pair_combinations)
        sorted_ordering = jnp.argsort(-(rank_values + extra_credit), stable=True)[:PAIR_SLOTS_LIMIT].astype(jnp.int32)
        least = max(TSET, PAIR_SLOTS_LIMIT // 4)
        count = jax.random.randint(jax.random.fold_in(sub_key, 3), (), least, PAIR_SLOTS_LIMIT + 1)
        count = jnp.where(device == full_device, PAIR_SLOTS_LIMIT, count)
        row_at = device // col_count
        col_at = device % col_count
        tgt_local = sorted_ordering // SSET
        src_local = sorted_ordering % SSET
        target = (tgt_local // BPD * col_count + col_at) * BPD + tgt_local % BPD
        source = (row_at * col_count + src_local // BPD) * BPD + src_local % BPD
        alive = jnp.arange(PAIR_SLOTS_LIMIT, dtype=jnp.int32) < count
        return jnp.stack([jnp.where(alive, target, -1), jnp.where(alive, source, -1)], axis=-1)
    table = jax.vmap(per_device)(jnp.arange(device_count, dtype=jnp.int32))
    return table.reshape(NPAIRS, 2).astype(jnp.int32)


def block_levels(rng, extent, cuts, low, high):
    def one(axis_at, parts):
        draws = jax.random.uniform(jax.random.fold_in(jax.random.fold_in(rng, 6), axis_at), (parts,), jnp.float32, low / len(cuts), high / len(cuts))
        return jnp.repeat(jnp.exp(draws), extent[axis_at] // parts).reshape((-1,) + (1,) * (len(extent) - axis_at - 1))

    factor_of = one(*cuts[0])
    for cut in cuts[1:]:
        factor_of = factor_of * one(*cut)
    return factor_of


def scatter_about(key, extent, width, limit, pieces=(), kind=jnp.bfloat16):
    drawn = jax.random.normal(key, extent, jnp.float32) * width
    if len(pieces) > 0:
        drawn = block_levels(key, extent, pieces, -0.22, 0.18) * drawn
    return jnp.clip(drawn, min=-limit, max=limit).astype(kind)


def setup_inputs(seed: int = 0) -> dict:
    arg_keys = jax.random.split(jax.random.key(seed), 4)
    return {
        "places": draw_places(jax.random.fold_in(arg_keys[3], 71), 0),
        "omega": scatter_about(arg_keys[1], (NB, RANK, BLK), 1.0, 6.0, ((0, 256),)),
        "pairs": draw_pairs(jax.random.fold_in(arg_keys[3], 71), 0),
    }


soft_sq = 0.09
ridge = 0.05

def kernel_tile(target_spots, source_spots):
    dist_sq = (target_spots[..., 0, :, None] - source_spots[..., 0, None, :]) ** 2
    dist_sq = dist_sq + (target_spots[..., 1, :, None] - source_spots[..., 1, None, :]) ** 2
    dist_sq = dist_sq + (target_spots[..., 2, :, None] - source_spots[..., 2, None, :]) ** 2
    return (source_spots[..., 3, None, :] * lax.rsqrt(dist_sq + soft_sq)).astype(jnp.bfloat16)

def factor(sketch):
    gram = jnp.einsum('tri,tsi->trs', sketch, sketch, precision=lax.Precision.HIGHEST)
    energy = lax.optimization_barrier(jnp.sum(sketch * sketch, axis=(1, 2)))
    shift = ridge * energy / sketch.shape[1]
    gram = gram + shift[:, None, None] * jnp.eye(sketch.shape[1], dtype=sketch.dtype)[None, :, :]
    lower = jnp.linalg.cholesky(gram)
    return lax.linalg.triangular_solve(lower, sketch, left_side=True, lower=True)

def reference(places, omega, pairs):
    live = pairs[:, 0] >= 0
    targets = jnp.where(live, pairs[:, 0], 0).astype(jnp.int32).reshape(-1, 16)
    sources = jnp.where(live, pairs[:, 1], 0).astype(jnp.int32).reshape(-1, 16)
    weight = live.astype(jnp.float32).reshape(-1, 16)

    def sketch_step(total, item):
        tgt_ids, source_numbers, alive = item
        kernel = kernel_tile(places[tgt_ids], places[source_numbers])
        contrib = jnp.einsum('prj,pij->pri', omega[source_numbers].astype(jnp.float32), kernel.astype(jnp.float32))
        return (total.at[tgt_ids].add(contrib * alive[:, None, None]), None)
    start_sum = jnp.zeros((places.shape[0], RANK, BLK), jnp.float32)
    sketch = lax.scan(sketch_step, start_sum, (targets, sources, weight))[0]
    basis = factor(sketch)
    bases = basis * math.sqrt(BLK)
    basis_b = basis.astype(jnp.bfloat16)

    def project(carry, item):
        tgt_ids, source_numbers, alive = item
        kernel = kernel_tile(places[tgt_ids], places[source_numbers])
        result = jnp.einsum('pri,pij->prj', basis_b[tgt_ids].astype(jnp.float32), kernel.astype(jnp.float32))
        return (carry, (result * alive[:, None, None]).astype(jnp.bfloat16))
    coeffs = lax.scan(project, jnp.zeros((), jnp.float32), (targets, sources, weight))[1]
    return (bases, coeffs.reshape(-1, RANK, BLK))
```

```python
import functools
import math

import jax
import jax.numpy as jnp
from jax import lax
from jax.experimental import pallas as pl
from jax.experimental.pallas import tpu as pltpu
from jax.sharding import PartitionSpec as P

soft_sq = 0.09
ridge = 0.05
MESH = pl.DeviceIdType.MESH
VMEM = pltpu.VMEM
GROUP = 4


def gather_kernel(rows, cols, places_ref, omega_ref, tgt_ref, src_ref, omegas_ref,
                  own_sem, row_send, row_recv, col_send, col_recv, om_send, om_recv):
    row, col = lax.axis_index("row"), lax.axis_index("col")
    barrier = pltpu.get_barrier_semaphore()
    for k in range(1, cols):
        pl.semaphore_signal(barrier, inc=1, device_id=(row, lax.rem(col + k, cols)), device_id_type=MESH)
    for k in range(1, rows):
        pl.semaphore_signal(barrier, inc=1, device_id=(lax.rem(row + k, rows), col), device_id_type=MESH)
    own = [
        pltpu.make_async_copy(places_ref, tgt_ref.at[pl.ds(row, 1)], own_sem.at[0]),
        pltpu.make_async_copy(places_ref, src_ref.at[pl.ds(col, 1)], own_sem.at[1]),
        pltpu.make_async_copy(omega_ref, omegas_ref.at[pl.ds(col, 1)], own_sem.at[2]),
    ]
    for c in own:
        c.start()
    pl.semaphore_wait(barrier, rows + cols - 2)

    def row_copy(k, slot):
        return pltpu.make_async_remote_copy(
            src_ref=places_ref, dst_ref=tgt_ref.at[pl.ds(slot, 1)], send_sem=row_send.at[k],
            recv_sem=row_recv.at[k], device_id=(lax.rem(row + k, rows), col), device_id_type=MESH)

    def col_copy(k, slot):
        return pltpu.make_async_remote_copy(
            src_ref=places_ref, dst_ref=src_ref.at[pl.ds(slot, 1)], send_sem=col_send.at[k],
            recv_sem=col_recv.at[k], device_id=(row, lax.rem(col + k, cols)), device_id_type=MESH)

    def om_copy(k, slot):
        return pltpu.make_async_remote_copy(
            src_ref=omega_ref, dst_ref=omegas_ref.at[pl.ds(slot, 1)], send_sem=om_send.at[k],
            recv_sem=om_recv.at[k], device_id=(row, lax.rem(col + k, cols)), device_id_type=MESH)

    for k in range(1, cols):
        col_copy(k, col).start()
    for k in range(1, rows):
        row_copy(k, row).start()
    for k in range(1, cols):
        om_copy(k, col).start()
    for c in own:
        c.wait()
    for k in range(1, cols):
        col_copy(k, lax.rem(col + cols - k, cols)).wait()
        om_copy(k, lax.rem(col + cols - k, cols)).wait()
    for k in range(1, rows):
        row_copy(k, lax.rem(row + rows - k, rows)).wait()


def gather_all(places, omega, rows, cols):
    return pl.pallas_call(
        functools.partial(gather_kernel, rows, cols),
        out_shape=[
            jax.ShapeDtypeStruct((rows,) + places.shape[1:], places.dtype),
            jax.ShapeDtypeStruct((cols,) + places.shape[1:], places.dtype),
            jax.ShapeDtypeStruct((cols,) + omega.shape[1:], omega.dtype),
        ],
        in_specs=[pl.BlockSpec(memory_space=VMEM)] * 2,
        out_specs=[pl.BlockSpec(memory_space=VMEM)] * 3,
        scratch_shapes=[
            pltpu.SemaphoreType.DMA((3,)),
            pltpu.SemaphoreType.DMA((rows,)), pltpu.SemaphoreType.DMA((rows,)),
            pltpu.SemaphoreType.DMA((cols,)), pltpu.SemaphoreType.DMA((cols,)),
            pltpu.SemaphoreType.DMA((cols,)), pltpu.SemaphoreType.DMA((cols,)),
        ],
        compiler_params=pltpu.CompilerParams(collective_id=0, has_side_effects=True),
        name="gather_all",
    )(places, omega)


def split(x):
    hi = x.astype(jnp.bfloat16)
    rest = x - hi.astype(jnp.float32)
    mid = rest.astype(jnp.bfloat16)
    low = (rest - mid.astype(jnp.float32)).astype(jnp.bfloat16)
    return hi, mid, low


def target_features(spots, row8):
    n = spots.shape[1]
    coords = jnp.concatenate([spots[0:3], jnp.zeros((5, n), jnp.float32)], axis=0)
    centre = jnp.sum(coords, axis=1, keepdims=True) * (1.0 / n)
    moved = coords - centre
    norm = jnp.sum(moved * moved, axis=0, keepdims=True) + soft_sq
    feats = jnp.where(row8 == 3, norm, jnp.where(row8 == 4, 1.0, -2.0 * moved))
    hi, mid, low = (v.astype(jnp.float32) for v in split(feats))
    stack = jnp.concatenate([hi, mid, low, hi, mid, hi], axis=0)
    return stack.T.astype(jnp.bfloat16), centre


def source_features(base, scale, centre, row8):
    moved = base - centre
    norm = jnp.sum(moved * moved, axis=0, keepdims=True)
    feats = scale * jnp.where(row8 == 3, 1.0, jnp.where(row8 == 4, norm, moved))
    hi, mid, low = (v.astype(jnp.float32) for v in split(feats))
    return jnp.concatenate([hi, hi, hi, mid, mid, low], axis=0).astype(jnp.bfloat16)


def tile_kernel(codes_ref, tgt_ref, src_ref, omegas_ref, tiles_ref, sketch_ref,
                feat_ref, centre_ref, base_ref, scale_ref):
    step = pl.program_id(0)
    tgt_count, src_count = tgt_ref.shape[0], src_ref.shape[0]
    n = tgt_ref.shape[2]
    row8 = lax.broadcasted_iota(jnp.int32, (8, n), 0)

    @pl.when(step == 0)
    def _():
        sketch_ref[...] = jnp.zeros_like(sketch_ref)

        def prepare_target(t, carry):
            feats, centre = target_features(tgt_ref[t], row8)
            feat_ref[t] = feats
            centre_ref[t] = jnp.broadcast_to(centre, (8, n))
            return carry

        def prepare_source(s, carry):
            spots = src_ref[s]
            base_ref[s] = jnp.concatenate([spots[0:3], jnp.zeros((5, n), jnp.float32)], axis=0)
            weight = spots[3:4]
            scale_ref[s] = jnp.broadcast_to(1.0 / (weight * weight), (8, n))
            return carry

        lax.fori_loop(0, tgt_count, prepare_target, 0)
        lax.fori_loop(0, src_count, prepare_source, 0)

    @pl.when(codes_ref[step * GROUP] >= 0)
    def _():
        for g in range(GROUP):
            code = codes_ref[step * GROUP + g]
            live = (code >= 0).astype(jnp.float32)
            code = jnp.maximum(code, 0)
            t, s = code // src_count, code % src_count
            source = source_features(base_ref[s], scale_ref[s], centre_ref[t], row8)
            dist = jnp.dot(feat_ref[t], source, preferred_element_type=jnp.float32)
            tile = lax.rsqrt(dist).astype(jnp.bfloat16)
            tiles_ref[g] = tile
            part = lax.dot_general(omegas_ref[s], tile, (((1,), (1,)), ((), ())),
                                   preferred_element_type=jnp.float32)
            sketch_ref[t] += part * live


def tiles_and_sketch(codes, tgt, src, omegas):
    slots = codes.shape[0]
    tgt_count, src_count, n = tgt.shape[0], src.shape[0], tgt.shape[2]
    rank = omegas.shape[1]
    steps = slots // GROUP
    grid_spec = pltpu.PrefetchScalarGridSpec(
        num_scalar_prefetch=1,
        grid=(steps,),
        in_specs=[pl.BlockSpec(memory_space=VMEM)] * 3,
        out_specs=[
            pl.BlockSpec((GROUP, n, n), lambda i, codes: (jnp.where(codes[i * GROUP] >= 0, i, steps), 0, 0)),
            pl.BlockSpec(memory_space=VMEM),
        ],
        scratch_shapes=[
            VMEM((tgt_count, n, 48), jnp.bfloat16), VMEM((tgt_count, 8, n), jnp.float32),
            VMEM((src_count, 8, n), jnp.float32), VMEM((src_count, 8, n), jnp.float32),
        ],
    )
    return pl.pallas_call(
        tile_kernel,
        grid_spec=grid_spec,
        out_shape=[
            jax.ShapeDtypeStruct((slots + GROUP, n, n), jnp.bfloat16),
            jax.ShapeDtypeStruct((tgt_count, rank, n), jnp.float32),
        ],
        compiler_params=pltpu.CompilerParams(vmem_limit_bytes=40 << 20),
        name="tiles_and_sketch",
    )(codes, tgt, src, omegas)


def factor(sketch, left, out):
    rank = sketch.shape[0]
    gram = lax.dot_general(sketch, sketch, (((1,), (1,)), ((), ())),
                           precision=lax.Precision.HIGHEST, preferred_element_type=jnp.float32)
    energy = jnp.sum(jnp.sum(sketch * sketch, axis=0, keepdims=True), axis=1, keepdims=True)
    shift = ridge * energy / rank
    eye = (lax.broadcasted_iota(jnp.int32, (rank, rank), 0)
           == lax.broadcasted_iota(jnp.int32, (rank, rank), 1))
    mat = gram + jnp.where(eye, shift, 0.0)
    for b in range(0, rank, 8):
        rows = rank - b
        width = sketch.shape[1]
        row_at = lax.broadcasted_iota(jnp.int32, (rows, 1), 0)
        columns = [jnp.broadcast_to(mat[:, b + j:b + j + 1], (rows, 128)) for j in range(8)]
        for k in range(8):
            inv = lax.rsqrt(columns[k][k:k + 1, :])
            inv_wide = jnp.concatenate([inv] * (width // 128), axis=1)
            mult = jnp.where(row_at > k, columns[k] * inv, 0.0)
            mult_wide = jnp.concatenate([mult] * (width // 128), axis=1)
            mat_row = mat[k:k + 1, :] * inv[:, :rank]
            sketch_row = sketch[k:k + 1, :] * inv_wide
            out[b + k:b + k + 1, :] = sketch_row
            for j in range(k + 1, 8):
                columns[j] = columns[j] - mult * (columns[j][k:k + 1, :] * inv)
            mat = mat - mult[:, :rank] * mat_row
            sketch = sketch - mult_wide * sketch_row
        mat, sketch = mat[8:], sketch[8:]


def reduce_kernel(rows, sketch_ref, bases_ref, all_ref, pair_ref, sum_ref, far_ref, basis_ref,
                  pair_sem, far_send, far_recv, own_sem, out_send, out_recv):
    row, col = lax.axis_index("row"), lax.axis_index("col")
    core = lax.rem(row, 2)
    chip = row // 2
    chips = rows // 2
    partner = row + 1 - 2 * core
    barrier = pltpu.get_barrier_semaphore()
    for k in range(1, rows):
        pl.semaphore_signal(barrier, inc=1, device_id=(lax.rem(row + k, rows), col), device_id_type=MESH)
    pl.semaphore_wait(barrier, rows - 1)

    swap = pltpu.make_async_remote_copy(
        src_ref=sketch_ref.at[:, 1 - core], dst_ref=pair_ref, send_sem=pair_sem.at[0],
        recv_sem=pair_sem.at[1], device_id=(partner, col), device_id_type=MESH)
    swap.start()
    swap.wait()

    def far_copy(k, slot):
        peer = lax.rem(chip + k, chips)
        return pltpu.make_async_remote_copy(
            src_ref=sum_ref.at[peer], dst_ref=far_ref.at[slot], send_sem=far_send.at[k],
            recv_sem=far_recv.at[k], device_id=(peer * 2 + core, col), device_id_type=MESH)

    for k in range(1, chips):
        peer = lax.rem(chip + k, chips)
        sum_ref[peer] = sketch_ref[peer, core] + pair_ref[peer]
        far_copy(k, k).start()
    total = sketch_ref[chip, core] + pair_ref[chip]
    for k in range(1, chips):
        far_copy(k, k).wait_recv()
        total += far_ref[k]
    factor(total, None, basis_ref)
    basis = basis_ref[...]
    bases_ref[0] = basis * math.sqrt(basis.shape[1])
    all_ref[row] = basis.astype(jnp.bfloat16)

    def out_copy(k, slot):
        return pltpu.make_async_remote_copy(
            src_ref=all_ref.at[slot], dst_ref=all_ref.at[slot], send_sem=out_send.at[k],
            recv_sem=out_recv.at[k], device_id=(lax.rem(row + k, rows), col), device_id_type=MESH)

    for k in range(1, rows):
        out_copy(k, row).start()
    for k in range(1, chips):
        far_copy(k, k).wait_send()
    for k in range(1, rows):
        out_copy(k, row).wait_send()
        out_copy(k, lax.rem(row + rows - k, rows)).wait_recv()


def reduce_and_factor(sketch):
    rows, rank, n = sketch.shape
    return pl.pallas_call(
        functools.partial(reduce_kernel, rows),
        out_shape=[
            jax.ShapeDtypeStruct((1, rank, n), jnp.float32),
            jax.ShapeDtypeStruct((rows, rank, n), jnp.bfloat16),
        ],
        in_specs=[pl.BlockSpec(memory_space=VMEM)],
        out_specs=[pl.BlockSpec(memory_space=VMEM)] * 2,
        scratch_shapes=[
            VMEM((rows // 2, rank, n), jnp.float32),
            VMEM((rows // 2, rank, n), jnp.float32),
            VMEM((rows // 2, rank, n), jnp.float32),
            VMEM((rank, n), jnp.float32),
            pltpu.SemaphoreType.DMA((2,)),
            pltpu.SemaphoreType.DMA((rows // 2,)), pltpu.SemaphoreType.DMA((rows // 2,)),
            pltpu.SemaphoreType.DMA((1,)),
            pltpu.SemaphoreType.DMA((rows,)), pltpu.SemaphoreType.DMA((rows,)),
        ],
        compiler_params=pltpu.CompilerParams(collective_id=1, has_side_effects=True,
                                             vmem_limit_bytes=16 << 20),
        name="reduce_and_factor",
    )(sketch.reshape(rows // 2, 2, rank, n))


def project_kernel(codes_ref, tiles_ref, basis_ref, out_ref):
    step = pl.program_id(0)
    src_count = basis_ref.shape[0]
    first_live = codes_ref[step * GROUP] >= 0

    @pl.when(first_live)
    def _():
        for g in range(GROUP):
            code = codes_ref[step * GROUP + g]
            live = (code >= 0).astype(jnp.float32)
            t = jnp.maximum(code, 0) // src_count
            result = jnp.dot(basis_ref[t], tiles_ref[g], preferred_element_type=jnp.float32)
            out_ref[g] = (result * live).astype(jnp.bfloat16)

    @pl.when(jnp.logical_not(first_live))
    def _():
        out_ref[...] = jnp.zeros_like(out_ref)


def project(codes, tiles, basis_all):
    slots = codes.shape[0]
    rank, n = basis_all.shape[1], basis_all.shape[2]
    grid_spec = pltpu.PrefetchScalarGridSpec(
        num_scalar_prefetch=1,
        grid=(slots // GROUP,),
        in_specs=[
            pl.BlockSpec((GROUP, n, n), lambda i, codes: (jnp.where(codes[i * GROUP] >= 0, i, 0), 0, 0)),
            pl.BlockSpec(memory_space=VMEM),
        ],
        out_specs=pl.BlockSpec((GROUP, rank, n), lambda i, codes: (i, 0, 0)),
    )
    return pl.pallas_call(
        project_kernel,
        grid_spec=grid_spec,
        out_shape=jax.ShapeDtypeStruct((slots, rank, n), jnp.bfloat16),
        compiler_params=pltpu.CompilerParams(vmem_limit_bytes=24 << 20),
        name="project",
    )(codes, tiles, basis_all)


def body(places, omega, pairs):
    rows, cols = lax.axis_size("row"), lax.axis_size("col")
    codes = jnp.where(pairs[:, 0] >= 0, pairs[:, 0] // cols * cols + pairs[:, 1] % cols, -1)
    tgt, src, omegas = gather_all(places, omega, rows, cols)
    tiles, sketch = tiles_and_sketch(codes, tgt, src, omegas)
    bases, basis_all = reduce_and_factor(sketch)
    coeffs = project(codes, tiles, basis_all)
    return (bases, coeffs)


def solution(mesh):
    in_specs = (
        P(("row", "col"), None, None),
        P(("row", "col"), None, None),
        P(("row", "col"), None),
    )
    out_specs = (P(("row", "col"), None, None), P(("row", "col"), None, None))
    return jax.shard_map(body, mesh=mesh, in_specs=in_specs, out_specs=out_specs, check_vma=False)
```

```python
import functools
import math

import jax
import jax.numpy as jnp
from jax import lax
from jax.experimental import pallas as pl
from jax.experimental.pallas import tpu as pltpu
from jax.sharding import PartitionSpec as P

soft_sq = 0.09
ridge = 0.05
MESH = pl.DeviceIdType.MESH
VMEM = pltpu.VMEM
SMEM = pltpu.SMEM
DMA = pltpu.SemaphoreType.DMA
GROUP = 8
NT = (((1,), (1,)), ((), ()))


def slots_kernel(cols, pairs_ref, meta_ref):
    slots = pairs_ref.shape[1]
    tgt_row = jnp.broadcast_to(pairs_ref[0:1], (slots, slots))
    src_row = jnp.broadcast_to(pairs_ref[1:2], (8, slots))
    tgt = tgt_row.T
    at_col = lax.broadcasted_iota(jnp.int32, (slots, slots), 0)
    at_row = lax.broadcasted_iota(jnp.int32, (slots, slots), 1)
    same = (tgt == tgt_row) & (tgt >= 0) & (at_col < at_row)
    last_of = (tgt >= 0) & (tgt // cols == at_row)

    def top(mask):
        best = jnp.where(mask, at_col, -1)
        rows = slots
        while rows > 8:
            rows //= 2
            best = jnp.maximum(best[:rows], best[rows:])
        for shift in (4, 2, 1):
            best = jnp.maximum(best, pltpu.roll(best, shift, 0))
        return jnp.where(best < 0, slots, best)

    live = tgt_row[0:8] >= 0
    code = jnp.where(live, tgt_row[0:8] // cols * cols + src_row % cols, 0)
    row = lax.broadcasted_iota(jnp.int32, (8, slots), 0)
    meta = jnp.where(row == 0, code, jnp.where(row == 1, top(same), top(last_of)))
    meta_ref[...] = jnp.where(row == 3, live.astype(jnp.int32), meta)


def slot_table(pairs, cols):
    return pl.pallas_call(
        functools.partial(slots_kernel, cols),
        out_shape=jax.ShapeDtypeStruct((8, pairs.shape[1]), jnp.int32),
        in_specs=[pl.BlockSpec(memory_space=VMEM)],
        out_specs=pl.BlockSpec(memory_space=VMEM),
        name="slot_table",
    )(pairs)


def split(x):
    hi = x.astype(jnp.bfloat16).astype(jnp.float32)
    rest = x - hi
    mid = rest.astype(jnp.bfloat16).astype(jnp.float32)
    return hi, mid, rest - mid


def target_features(spots, row8):
    n = spots.shape[1]
    coords = jnp.concatenate([spots[0:3], jnp.zeros((5, n), jnp.float32)], axis=0)
    centre = jnp.sum(coords, axis=1, keepdims=True) * (1.0 / n)
    moved = coords - centre
    norm = jnp.sum(moved * moved, axis=0, keepdims=True) + soft_sq
    feats = jnp.where(row8 == 3, norm, jnp.where(row8 == 4, 1.0, -2.0 * moved))
    hi, mid, low = split(feats)
    stack = jnp.concatenate([hi, mid, low, hi, mid, hi], axis=0)
    return stack.T.astype(jnp.bfloat16), centre


def source_features(base, scale, centre, row8):
    moved = base - centre
    norm = jnp.sum(moved * moved, axis=0, keepdims=True)
    feats = scale * jnp.where(row8 == 3, 1.0, jnp.where(row8 == 4, norm, moved))
    hi, mid, low = split(feats)
    return jnp.concatenate([hi, hi, hi, mid, mid, low], axis=0).astype(jnp.bfloat16)


def prepare(tgt_ref, src_ref, feat_ref, centre_ref, base_ref, scale_ref):
    n = tgt_ref.shape[2]
    row8 = lax.broadcasted_iota(jnp.int32, (8, n), 0)

    def prepare_target(t, carry):
        feats, centre = target_features(tgt_ref[t], row8)
        feat_ref[t] = feats
        centre_ref[t] = jnp.broadcast_to(centre, (8, n))
        return carry

    def prepare_source(s, carry):
        spots = src_ref[s]
        base_ref[s] = jnp.concatenate([spots[0:3], jnp.zeros((5, n), jnp.float32)], axis=0)
        weight = spots[3:4]
        scale_ref[s] = jnp.broadcast_to(1.0 / (weight * weight), (8, n))
        return carry

    lax.fori_loop(0, tgt_ref.shape[0], prepare_target, 0, unroll=4)
    lax.fori_loop(0, src_ref.shape[0], prepare_source, 0, unroll=4)


def tile_group(first, cols, meta_ref, feat_ref, centre_ref, base_ref, scale_ref, tiles_ref):
    n = feat_ref.shape[1]
    row8 = lax.broadcasted_iota(jnp.int32, (8, n), 0)
    for g in range(GROUP):
        code = meta_ref[0, first + g]
        t, s = code // cols, code % cols
        source = source_features(base_ref[s], scale_ref[s], centre_ref[t], row8)
        dist = jnp.dot(feat_ref[t], source, preferred_element_type=jnp.float32)
        tiles_ref[first + g] = lax.rsqrt(dist).astype(jnp.bfloat16)


def sketch_group(first, cols, meta_ref, omegas_ref, tiles_ref, running_ref):
    parts = []
    for g in range(GROUP):
        s = meta_ref[0, first + g] % cols
        live = meta_ref[3, first + g].astype(jnp.float32)
        part = lax.dot_general(omegas_ref[s], tiles_ref[first + g], NT, preferred_element_type=jnp.float32)
        parts.append(part * live)
    for g in range(GROUP):
        running_ref[first + g] = running_ref[meta_ref[1, first + g]] + parts[g]


def factor(sketch, out):
    rank, width = sketch.shape
    gram = lax.dot_general(sketch, sketch, NT, precision=lax.Precision.HIGHEST,
                           preferred_element_type=jnp.float32)
    energy = jnp.sum(jnp.sum(sketch * sketch, axis=0, keepdims=True), axis=1, keepdims=True)
    shift = ridge * energy / rank
    eye = (lax.broadcasted_iota(jnp.int32, (rank, rank), 0)
           == lax.broadcasted_iota(jnp.int32, (rank, rank), 1))
    mat = gram + jnp.where(eye, shift, 0.0)
    for b in range(0, rank, 8):
        rows = rank - b
        row_at = lax.broadcasted_iota(jnp.int32, (rows, 1), 0)
        columns = [jnp.broadcast_to(mat[:, b + j:b + j + 1], (rows, 128)) for j in range(8)]
        for k in range(8):
            inv = lax.rsqrt(columns[k][k:k + 1, :])
            inv_wide = jnp.concatenate([inv] * (width // 128), axis=1)
            mult = jnp.where(row_at > k, columns[k] * inv, 0.0)
            mult_wide = jnp.concatenate([mult] * (width // 128), axis=1)
            mat_row = mat[k:k + 1, :] * inv[:, :rank]
            sketch_row = sketch[k:k + 1, :] * inv_wide
            out[b + k:b + k + 1, :] = sketch_row
            for j in range(k + 1, 8):
                columns[j] = columns[j] - mult * (columns[j][k:k + 1, :] * inv)
            mat = mat - mult[:, :rank] * mat_row
            sketch = sketch - mult_wide * sketch_row
        mat, sketch = mat[8:], sketch[8:]


def sketch_kernel(rows, cols, meta_ref, places_ref, omega_ref, tiles_out, bases_ref, all_ref,
                  tgt_ref, src_ref, omegas_ref, feat_ref, centre_ref, base_ref, scale_ref,
                  tiles_ref, running_ref, stage_ref, pair_ref, sum_ref, far_ref, basis_ref,
                  own_sem, row_send, row_recv, col_send, col_recv, om_send, om_recv, tile_sem,
                  pair_send, pair_recv, far_send, far_recv, out_send, out_recv, relay_send, relay_recv):
    row, col = lax.axis_index("row"), lax.axis_index("col")
    core, chip, chips = lax.rem(row, 2), row // 2, rows // 2
    partner = row + 1 - 2 * core
    slots = tiles_ref.shape[0]
    groups = slots // GROUP

    barrier = pltpu.get_barrier_semaphore()
    for k in range(1, cols):
        pl.semaphore_signal(barrier, inc=1, device_id=(row, lax.rem(col + k, cols)), device_id_type=MESH)
    for k in range(1, rows):
        pl.semaphore_signal(barrier, inc=1, device_id=(lax.rem(row + k, rows), col), device_id_type=MESH)
    own = [
        pltpu.make_async_copy(places_ref, tgt_ref.at[pl.ds(row, 1)], own_sem.at[0]),
        pltpu.make_async_copy(places_ref, src_ref.at[pl.ds(col, 1)], own_sem.at[1]),
        pltpu.make_async_copy(omega_ref, omegas_ref.at[pl.ds(col, 1)], own_sem.at[2]),
    ]
    for c in own:
        c.start()
    running_ref[slots] = jnp.zeros_like(running_ref[slots])
    for c in own:
        c.wait()
    pl.semaphore_wait(barrier, rows + cols - 2)

    def row_copy(k, slot):
        return pltpu.make_async_remote_copy(
            src_ref=tgt_ref.at[pl.ds(row, 1)], dst_ref=tgt_ref.at[pl.ds(slot, 1)], send_sem=row_send.at[k],
            recv_sem=row_recv.at[k], device_id=(lax.rem(row + k, rows), col), device_id_type=MESH)

    def col_copy(k, slot):
        return pltpu.make_async_remote_copy(
            src_ref=src_ref.at[pl.ds(col, 1)], dst_ref=src_ref.at[pl.ds(slot, 1)], send_sem=col_send.at[k],
            recv_sem=col_recv.at[k], device_id=(row, lax.rem(col + k, cols)), device_id_type=MESH)

    def om_copy(k, slot):
        return pltpu.make_async_remote_copy(
            src_ref=omegas_ref.at[pl.ds(col, 1)], dst_ref=omegas_ref.at[pl.ds(slot, 1)], send_sem=om_send.at[k],
            recv_sem=om_recv.at[k], device_id=(row, lax.rem(col + k, cols)), device_id_type=MESH)

    for k in range(1, cols):
        col_copy(k, col).start()
    for k in range(1, rows):
        row_copy(k, row).start()
    for k in range(1, cols):
        om_copy(k, col).start()
    for k in range(1, rows):
        row_copy(k, lax.rem(row + rows - k, rows)).wait()
    for k in range(1, cols):
        col_copy(k, lax.rem(col + cols - k, cols)).wait()
    prepare(tgt_ref, src_ref, feat_ref, centre_ref, base_ref, scale_ref)

    def tile_copy(i):
        part = pl.ds(i * GROUP, GROUP)
        return pltpu.make_async_copy(tiles_ref.at[part], tiles_out.at[part], tile_sem.at[i])

    def tile_step(i, carry):
        tile_group(i * GROUP, cols, meta_ref, feat_ref, centre_ref, base_ref, scale_ref, tiles_ref)
        tile_copy(i).start()
        return carry

    lax.fori_loop(0, groups, tile_step, 0)
    for k in range(1, cols):
        om_copy(k, lax.rem(col + cols - k, cols)).wait()

    def sketch_step(i, carry):
        sketch_group(i * GROUP, cols, meta_ref, omegas_ref, tiles_ref, running_ref)
        return carry

    lax.fori_loop(0, groups, sketch_step, 0)

    def pair_copy(c):
        return pltpu.make_async_remote_copy(
            src_ref=stage_ref.at[c], dst_ref=pair_ref.at[c], send_sem=pair_send.at[c],
            recv_sem=pair_recv.at[c], device_id=(partner, col), device_id_type=MESH)

    half = chips // 2

    def far_chip(k):
        return lax.rem(chip // half + k // half, 2) * half + lax.rem(lax.rem(chip, half) + k % half, half)

    def back_chip(k):
        return lax.rem(chip // half + k // half, 2) * half + lax.rem(lax.rem(chip, half) + half - k % half, half)

    def far_copy(k):
        return pltpu.make_async_remote_copy(
            src_ref=sum_ref.at[k], dst_ref=far_ref.at[k], send_sem=far_send.at[k],
            recv_sem=far_recv.at[k], device_id=(far_chip(k) * 2 + core, col), device_id_type=MESH)

    order = sorted(range(1, chips), key=lambda k: -(k // half + min(k % half, half - k % half)))
    for k in order + [0]:
        c = far_chip(k)
        stage_ref[c] = running_ref[meta_ref[2, 2 * c + 1 - core]]
        pair_copy(c).start()
    for k in order + [0]:
        c = far_chip(k)
        sum_ref[k] = running_ref[meta_ref[2, 2 * c + core]]
    for k in order + [0]:
        c = far_chip(k)
        pair_copy(c).wait_recv()
        sum_ref[k] += pair_ref[c]
        if k:
            far_copy(k).start()
    total = sum_ref[0]
    for k in reversed(order):
        far_copy(k).wait_recv()
        total += far_ref[k]
    factor(total, basis_ref)
    basis = basis_ref[...]
    all_ref[row] = basis.astype(jnp.bfloat16)

    def out_copy(k, slot):
        return pltpu.make_async_remote_copy(
            src_ref=all_ref.at[slot], dst_ref=all_ref.at[slot], send_sem=out_send.at[k],
            recv_sem=out_recv.at[k], device_id=(far_chip(k) * 2 + core, col), device_id_type=MESH)

    def relay_copy(k, slot):
        return pltpu.make_async_remote_copy(
            src_ref=all_ref.at[slot], dst_ref=all_ref.at[slot], send_sem=relay_send.at[k],
            recv_sem=relay_recv.at[k], device_id=(partner, col), device_id_type=MESH)

    for k in order:
        out_copy(k, row).start()
    relay_copy(0, row).start()
    bases_ref[0] = basis * math.sqrt(basis.shape[1])
    for c in range(chips):
        pair_copy(c).wait_send()
    for k in order:
        far_copy(k).wait_send()
    for i in range(groups):
        tile_copy(i).wait()
    for k in reversed(order):
        slot = back_chip(k) * 2 + core
        out_copy(k, slot).wait_recv()
        relay_copy(k, slot).start()
    for k in order:
        out_copy(k, row).wait_send()
    for k in [0] + order[::-1]:
        slot = back_chip(k) * 2 + core
        relay_copy(k, slot).wait_send()
        relay_copy(k, slot + 1 - 2 * core).wait_recv()


def sketch_and_factor(meta, places, omega, rows, cols):
    slots = meta.shape[1]
    rank, n = omega.shape[1], omega.shape[2]
    chips = rows // 2
    bf16, f32 = jnp.bfloat16, jnp.float32
    return pl.pallas_call(
        functools.partial(sketch_kernel, rows, cols),
        out_shape=[
            jax.ShapeDtypeStruct((slots, n, n), bf16),
            jax.ShapeDtypeStruct((1, rank, n), f32),
            jax.ShapeDtypeStruct((rows, rank, n), bf16),
        ],
        in_specs=[pl.BlockSpec(memory_space=SMEM)] + [pl.BlockSpec(memory_space=pl.ANY)] * 2,
        out_specs=[pl.BlockSpec(memory_space=pl.ANY)] + [pl.BlockSpec(memory_space=VMEM)] * 2,
        scratch_shapes=[
            VMEM((rows,) + places.shape[1:], f32), VMEM((cols,) + places.shape[1:], f32),
            VMEM((cols, rank, n), bf16),
            VMEM((rows, n, 48), bf16), VMEM((rows, 8, n), f32),
            VMEM((cols, 8, n), f32), VMEM((cols, 8, n), f32),
            VMEM((slots, n, n), bf16), VMEM((slots + 1, rank, n), f32),
            VMEM((chips, rank, n), f32), VMEM((chips, rank, n), f32),
            VMEM((chips, rank, n), f32), VMEM((chips, rank, n), f32),
            VMEM((rank, n), f32),
            DMA((3,)), DMA((rows,)), DMA((rows,)), DMA((cols,)), DMA((cols,)), DMA((cols,)), DMA((cols,)),
            DMA((slots // GROUP,)),
            DMA((chips,)), DMA((chips,)), DMA((chips,)), DMA((chips,)),
            DMA((chips,)), DMA((chips,)), DMA((chips,)), DMA((chips,)),
        ],
        compiler_params=pltpu.CompilerParams(collective_id=0, has_side_effects=True,
                                             vmem_limit_bytes=60 << 20),
        name="sketch_and_factor",
    )(meta, places, omega)


def project_kernel(cols, meta_ref, basis_ref, tiles_hbm, out_hbm, tiles_ref, out_ref, in_sem, out_sem):
    slots = tiles_ref.shape[0]
    groups = slots // GROUP

    def tile_copy(i):
        part = pl.ds(i * GROUP, GROUP)
        return pltpu.make_async_copy(tiles_hbm.at[part], tiles_ref.at[part], in_sem.at[i])

    def out_copy(i):
        part = pl.ds(i * GROUP, GROUP)
        return pltpu.make_async_copy(out_ref.at[part], out_hbm.at[part], out_sem.at[i])

    def start(i, carry):
        tile_copy(i).start()
        return carry

    def step(i, carry):
        tile_copy(i).wait()
        for g in range(GROUP):
            p = i * GROUP + g
            live = meta_ref[3, p].astype(jnp.float32)
            result = jnp.dot(basis_ref[meta_ref[0, p] // cols], tiles_ref[p],
                             preferred_element_type=jnp.float32)
            out_ref[p] = (result * live).astype(jnp.bfloat16)
        out_copy(i).start()
        return carry

    def finish(i, carry):
        out_copy(i).wait()
        return carry

    lax.fori_loop(0, groups, start, 0)
    lax.fori_loop(0, groups, step, 0)
    lax.fori_loop(0, groups, finish, 0)


def project(meta, tiles, basis_all, cols):
    slots = meta.shape[1]
    rank, n = basis_all.shape[1], basis_all.shape[2]
    return pl.pallas_call(
        functools.partial(project_kernel, cols),
        out_shape=jax.ShapeDtypeStruct((slots, rank, n), jnp.bfloat16),
        in_specs=[pl.BlockSpec(memory_space=SMEM), pl.BlockSpec(memory_space=VMEM),
                  pl.BlockSpec(memory_space=pl.ANY)],
        out_specs=pl.BlockSpec(memory_space=pl.ANY),
        scratch_shapes=[
            VMEM((slots, n, n), jnp.bfloat16), VMEM((slots, rank, n), jnp.bfloat16),
            DMA((slots // GROUP,)), DMA((slots // GROUP,)),
        ],
        compiler_params=pltpu.CompilerParams(vmem_limit_bytes=60 << 20),
        name="project",
    )(meta, basis_all, tiles)


def body(places, omega, pairs):
    rows, cols = lax.axis_size("row"), lax.axis_size("col")
    meta = slot_table(pairs.T, cols)
    tiles, bases, basis_all = sketch_and_factor(meta, places, omega, rows, cols)
    coeffs = project(meta, tiles, basis_all, cols)
    return (bases, coeffs)


def solution(mesh):
    in_specs = (
        P(("row", "col"), None, None),
        P(("row", "col"), None, None),
        P(("row", "col"), None),
    )
    out_specs = (P(("row", "col"), None, None), P(("row", "col"), None, None))
    return jax.shard_map(body, mesh=mesh, in_specs=in_specs, out_specs=out_specs, check_vma=False)
```

```python
import functools
import math

import jax
import jax.numpy as jnp
from jax import lax
from jax.experimental import pallas as pl
from jax.experimental.pallas import tpu as pltpu
from jax.sharding import PartitionSpec as P

soft_sq = 0.09
ridge = 0.05
MESH = pl.DeviceIdType.MESH
VMEM = pltpu.VMEM
SMEM = pltpu.SMEM
DMA = pltpu.SemaphoreType.DMA
GROUP = 16
NT = (((1,), (1,)), ((), ()))


def slot_table(cols, pairs_ref, meta_ref):
    slots = pairs_ref.shape[1]
    tgt_row = jnp.broadcast_to(pairs_ref[0:1], (slots, slots))
    src_row = jnp.broadcast_to(pairs_ref[1:2], (8, slots))
    tgt = tgt_row.T
    at_col = lax.broadcasted_iota(jnp.int32, (slots, slots), 0)
    at_row = lax.broadcasted_iota(jnp.int32, (slots, slots), 1)
    same = (tgt == tgt_row) & (tgt >= 0) & (at_col < at_row)
    last_of = (tgt >= 0) & (tgt // cols == at_row)

    def top(mask):
        best = jnp.where(mask, at_col, -1)
        rows = slots
        while rows > 8:
            rows //= 2
            best = jnp.maximum(best[:rows], best[rows:])
        for shift in (4, 2, 1):
            best = jnp.maximum(best, pltpu.roll(best, shift, 0))
        return jnp.where(best < 0, slots, best)

    live = tgt_row[0:8] >= 0
    code = jnp.where(live, tgt_row[0:8] // cols * cols + src_row % cols, 0)
    row = lax.broadcasted_iota(jnp.int32, (8, slots), 0)
    meta = jnp.where(row == 0, code, jnp.where(row == 1, top(same), top(last_of)))
    meta_ref[...] = jnp.where(row == 3, live.astype(jnp.int32), meta)


def split(x):
    hi = x.astype(jnp.bfloat16).astype(jnp.float32)
    rest = x - hi
    mid = rest.astype(jnp.bfloat16).astype(jnp.float32)
    return hi, mid, rest - mid


def target_features(spots, row8):
    n = spots.shape[1]
    coords = jnp.concatenate([spots[0:3], jnp.zeros((5, n), jnp.float32)], axis=0)
    centre = jnp.sum(coords, axis=1, keepdims=True) * (1.0 / n)
    moved = coords - centre
    norm = jnp.sum(moved * moved, axis=0, keepdims=True) + soft_sq
    feats = jnp.where(row8 == 3, norm, jnp.where(row8 == 4, 1.0, -2.0 * moved))
    hi, mid, low = split(feats)
    stack = jnp.concatenate([hi, mid, low, hi, mid, hi], axis=0)
    return stack.T.astype(jnp.bfloat16), centre


def source_features(base, scale, centre, row8):
    moved = base - centre
    norm = jnp.sum(moved * moved, axis=0, keepdims=True)
    feats = scale * jnp.where(row8 == 3, 1.0, jnp.where(row8 == 4, norm, moved))
    hi, mid, low = split(feats)
    return jnp.concatenate([hi, hi, hi, mid, mid, low], axis=0).astype(jnp.bfloat16)


def prepare_targets(tgt_ref, feat_ref, centre_ref):
    n = tgt_ref.shape[2]
    row8 = lax.broadcasted_iota(jnp.int32, (8, n), 0)

    def one(t, carry):
        feats, centre = target_features(tgt_ref[t], row8)
        feat_ref[t] = feats
        centre_ref[t] = jnp.broadcast_to(centre, (8, n))
        return carry

    lax.fori_loop(0, tgt_ref.shape[0], one, 0, unroll=4)


def prepare_sources(src_ref, base_ref, scale_ref):
    n = src_ref.shape[2]

    def one(s, carry):
        spots = src_ref[s]
        base_ref[s] = jnp.concatenate([spots[0:3], jnp.zeros((5, n), jnp.float32)], axis=0)
        weight = spots[3:4]
        scale_ref[s] = jnp.broadcast_to(1.0 / (weight * weight), (8, n))
        return carry

    lax.fori_loop(0, src_ref.shape[0], one, 0, unroll=4)


def tile_group(first, cols, meta_ref, feat_ref, centre_ref, base_ref, scale_ref, tiles_ref):
    n = feat_ref.shape[1]
    row8 = lax.broadcasted_iota(jnp.int32, (8, n), 0)
    for g in range(GROUP):
        code = meta_ref[0, first + g]
        t, s = code // cols, code % cols
        source = source_features(base_ref[s], scale_ref[s], centre_ref[t], row8)
        dist = jnp.dot(feat_ref[t], source, preferred_element_type=jnp.float32)
        tiles_ref[first + g] = lax.rsqrt(dist).astype(jnp.bfloat16)


def sketch_group(first, h, cols, meta_ref, omegas_ref, tiles_ref, running_ref):
    half = running_ref.shape[3]
    parts = []
    for g in range(GROUP):
        s = meta_ref[0, first + g] % cols
        live = meta_ref[3, first + g].astype(jnp.float32)
        part = lax.dot_general(omegas_ref[s], tiles_ref[first + g, h * half:(h + 1) * half], NT,
                               preferred_element_type=jnp.float32)
        parts.append(part * live)
    for g in range(GROUP):
        running_ref[h, first + g] = running_ref[h, meta_ref[1, first + g]] + parts[g]


def factor(sketch, out, at_half):
    rank, width = sketch.shape
    gram = lax.dot_general(sketch, sketch, NT, precision=lax.Precision.HIGHEST,
                           preferred_element_type=jnp.float32)
    energy = jnp.sum(jnp.sum(sketch * sketch, axis=0, keepdims=True), axis=1, keepdims=True)
    shift = ridge * energy / rank
    eye = (lax.broadcasted_iota(jnp.int32, (rank, rank), 0)
           == lax.broadcasted_iota(jnp.int32, (rank, rank), 1))
    mat = gram + jnp.where(eye, shift, 0.0)
    for b in range(0, rank, 8):
        rows = rank - b
        row_at = lax.broadcasted_iota(jnp.int32, (rows, 1), 0)
        columns = [jnp.broadcast_to(mat[:, b + j:b + j + 1], (rows, 128)) for j in range(8)]
        for k in range(8):
            inv = lax.rsqrt(columns[k][k:k + 1, :])
            inv_wide = jnp.concatenate([inv] * (width // 128), axis=1)
            mult = jnp.where(row_at > k, columns[k] * inv, 0.0)
            mult_wide = jnp.concatenate([mult] * (width // 128), axis=1)
            mat_row = mat[k:k + 1, :] * inv[:, :rank]
            sketch_row = sketch[k:k + 1, :] * inv_wide
            out[b + k:b + k + 1, :] = sketch_row
            for j in range(k + 1, 8):
                columns[j] = columns[j] - mult * (columns[j][k:k + 1, :] * inv)
            mat = mat - mult[:, :rank] * mat_row
            sketch = sketch - mult_wide * sketch_row
        mat, sketch = mat[8:], sketch[8:]
        if 2 * (b + 8) == rank:
            at_half()


def sketch_kernel(rows, cols, pairs_hbm, places_ref, omega_ref, tiles_ref, basis_ref, all_ref, table_ref,
                  pairs_ref, meta_ref, tgt_ref, src_ref, omegas_ref, feat_ref, centre_ref, base_ref, scale_ref,
                  running_ref, stage_ref, pair_ref, sum_ref, far_ref,
                  own_sem, row_send, row_recv, col_send, col_recv, om_send, om_recv,
                  pair_send, pair_recv, far_send, far_recv, out_send, out_recv, relay_send, relay_recv):
    row, col = lax.axis_index("row"), lax.axis_index("col")
    core, chip, chips = lax.rem(row, 2), row // 2, rows // 2
    partner = row + 1 - 2 * core
    slots = tiles_ref.shape[0]
    groups = slots // GROUP
    rank, half = running_ref.shape[2], running_ref.shape[3]
    ring, depth = chips // 2, cols // 2

    def moved(at, k, size):
        return lax.rem(at // size + k // size, 2) * size + lax.rem(lax.rem(at, size) + k % size, size)

    def moved_back(at, k, size):
        return lax.rem(at // size + k // size, 2) * size + lax.rem(lax.rem(at, size) + size - k % size, size)

    far = sorted(range(1, chips), key=lambda k: -(k // ring + min(k % ring, ring - k % ring)))
    deep = sorted(range(1, cols), key=lambda k: -(2 * (k // depth) + min(k % depth, depth - k % depth)))
    wide = [2 * k + c for k in far + [0] for c in (0, 1) if 2 * k + c]

    def row_at(k):
        return moved(chip, k // 2, ring) * 2 + lax.rem(core + k % 2, 2)

    def row_back(k):
        return moved_back(chip, k // 2, ring) * 2 + lax.rem(core + k % 2, 2)

    slot_copy = pltpu.make_async_copy(pairs_hbm, pairs_ref, own_sem.at[4])
    slot_copy.start()
    barrier = pltpu.get_barrier_semaphore()
    for k in deep:
        pl.semaphore_signal(barrier, inc=1, device_id=(row, moved(col, k, depth)), device_id_type=MESH)
    for k in wide:
        pl.semaphore_signal(barrier, inc=1, device_id=(row_at(k), col), device_id_type=MESH)
    own = [
        pltpu.make_async_copy(places_ref, tgt_ref.at[pl.ds(row, 1)], own_sem.at[0]),
        pltpu.make_async_copy(places_ref, src_ref.at[pl.ds(col, 1)], own_sem.at[1]),
        pltpu.make_async_copy(omega_ref, omegas_ref.at[pl.ds(col, 1)], own_sem.at[2]),
    ]
    for c in own:
        c.start()
    slot_copy.wait()
    slot_table(cols, pairs_ref, table_ref)
    table = pltpu.make_async_copy(table_ref, meta_ref, own_sem.at[3])
    table.start()
    for h in range(2):
        running_ref[h, slots] = jnp.zeros((rank, half), jnp.float32)
    for c in own:
        c.wait()
    table.wait()
    pl.semaphore_wait(barrier, rows + cols - 2)

    def row_copy(k, slot):
        return pltpu.make_async_remote_copy(
            src_ref=tgt_ref.at[pl.ds(row, 1)], dst_ref=tgt_ref.at[pl.ds(slot, 1)], send_sem=row_send.at[k],
            recv_sem=row_recv.at[k], device_id=(row_at(k), col), device_id_type=MESH)

    def col_copy(k, slot):
        return pltpu.make_async_remote_copy(
            src_ref=src_ref.at[pl.ds(col, 1)], dst_ref=src_ref.at[pl.ds(slot, 1)], send_sem=col_send.at[k],
            recv_sem=col_recv.at[k], device_id=(row, moved(col, k, depth)), device_id_type=MESH)

    def om_copy(k, slot):
        return pltpu.make_async_remote_copy(
            src_ref=omegas_ref.at[pl.ds(col, 1)], dst_ref=omegas_ref.at[pl.ds(slot, 1)], send_sem=om_send.at[k],
            recv_sem=om_recv.at[k], device_id=(row, moved(col, k, depth)), device_id_type=MESH)

    for k in deep:
        col_copy(k, col).start()
    for k in wide:
        row_copy(k, row).start()
    for k in deep:
        om_copy(k, col).start()
    for k in wide:
        row_copy(k, row_back(k)).wait()
    prepare_targets(tgt_ref, feat_ref, centre_ref)
    for k in deep:
        col_copy(k, moved_back(col, k, depth)).wait()
    prepare_sources(src_ref, base_ref, scale_ref)

    def tile_step(i, carry):
        tile_group(i * GROUP, cols, meta_ref, feat_ref, centre_ref, base_ref, scale_ref, tiles_ref)
        return carry

    lax.fori_loop(0, groups, tile_step, 0)
    for k in deep:
        om_copy(k, moved_back(col, k, depth)).wait()

    def pair_copy(h, k):
        return pltpu.make_async_remote_copy(
            src_ref=stage_ref.at[h, k], dst_ref=pair_ref.at[h, k], send_sem=pair_send.at[h, k],
            recv_sem=pair_recv.at[h, k], device_id=(partner, col), device_id_type=MESH)

    def far_copy(h, k):
        return pltpu.make_async_remote_copy(
            src_ref=sum_ref.at[h, k], dst_ref=far_ref.at[h, k], send_sem=far_send.at[h, k],
            recv_sem=far_recv.at[h, k], device_id=(moved(chip, k, ring) * 2 + core, col), device_id_type=MESH)

    for h in range(2):
        def sketch_step(i, carry, h=h):
            sketch_group(i * GROUP, h, cols, meta_ref, omegas_ref, tiles_ref, running_ref)
            return carry

        lax.fori_loop(0, groups, sketch_step, 0)
        for k in far + [0]:
            stage_ref[h, k] = running_ref[h, meta_ref[2, 2 * moved(chip, k, ring) + 1 - core]]
            pair_copy(h, k).start()
        for k in far + [0]:
            sum_ref[h, k] = running_ref[h, meta_ref[2, 2 * moved(chip, k, ring) + core]]
        for k in far + [0]:
            pair_copy(h, k).wait_recv()
            sum_ref[h, k] += pair_ref[h, k]
            if k:
                far_copy(h, k).start()

    totals = []
    for h in range(2):
        total = sum_ref[h, 0]
        for k in reversed(far):
            far_copy(h, k).wait_recv()
            total += far_ref[h, k]
        totals.append(total)

    part = rank // 2

    def out_copy(q, k, slot):
        block = all_ref.at[slot, pl.ds(q * part, part)]
        return pltpu.make_async_remote_copy(
            src_ref=block, dst_ref=block, send_sem=out_send.at[q, k], recv_sem=out_recv.at[q, k],
            device_id=(moved(chip, k, ring) * 2 + core, col), device_id_type=MESH)

    def relay_copy(q, k, slot):
        block = all_ref.at[slot, pl.ds(q * part, part)]
        return pltpu.make_async_remote_copy(
            src_ref=block, dst_ref=block, send_sem=relay_send.at[q, k], recv_sem=relay_recv.at[q, k],
            device_id=(partner, col), device_id_type=MESH)

    def send_part(q):
        block = pl.ds(q * part, part)
        all_ref[row, block] = basis_ref[0, block].astype(jnp.bfloat16)
        for k in far:
            out_copy(q, k, row).start()
        relay_copy(q, 0, row).start()

    factor(jnp.concatenate(totals, axis=1), basis_ref.at[0], lambda: send_part(0))
    send_part(1)
    for h in range(2):
        for k in far:
            pair_copy(h, k).wait_send()
            far_copy(h, k).wait_send()
        pair_copy(h, 0).wait_send()
    for q in range(2):
        for k in reversed(far):
            slot = moved_back(chip, k, ring) * 2 + core
            out_copy(q, k, slot).wait_recv()
            relay_copy(q, k, slot).start()
    for q in range(2):
        for k in far:
            out_copy(q, k, row).wait_send()
        for k in [0] + far[::-1]:
            slot = moved_back(chip, k, ring) * 2 + core
            relay_copy(q, k, slot).wait_send()
            relay_copy(q, k, slot + 1 - 2 * core).wait_recv()


def sketch_and_factor(pairs, places, omega, rows, cols):
    slots = pairs.shape[1]
    rank, n = omega.shape[1], omega.shape[2]
    chips = rows // 2
    bf16, f32 = jnp.bfloat16, jnp.float32
    return pl.pallas_call(
        functools.partial(sketch_kernel, rows, cols),
        out_shape=[
            jax.ShapeDtypeStruct((slots, n, n), bf16),
            jax.ShapeDtypeStruct((1, rank, n), f32),
            jax.ShapeDtypeStruct((rows, rank, n), bf16),
            jax.ShapeDtypeStruct((8, slots), jnp.int32),
        ],
        in_specs=[pl.BlockSpec(memory_space=pltpu.HBM)] * 3,
        out_specs=[pl.BlockSpec(memory_space=VMEM)] * 4,
        scratch_shapes=[
            VMEM((2, slots), jnp.int32), SMEM((8, slots), jnp.int32),
            VMEM((rows,) + places.shape[1:], f32), VMEM((cols,) + places.shape[1:], f32),
            VMEM((cols, rank, n), bf16),
            VMEM((rows, n, 48), bf16), VMEM((rows, 8, n), f32),
            VMEM((cols, 8, n), f32), VMEM((cols, 8, n), f32),
            VMEM((2, slots + 1, rank, n // 2), f32),
            VMEM((2, chips, rank, n // 2), f32), VMEM((2, chips, rank, n // 2), f32),
            VMEM((2, chips, rank, n // 2), f32), VMEM((2, chips, rank, n // 2), f32),
            DMA((5,)), DMA((rows,)), DMA((rows,)), DMA((cols,)), DMA((cols,)), DMA((cols,)), DMA((cols,)),
            DMA((2, chips)), DMA((2, chips)), DMA((2, chips)), DMA((2, chips)),
            DMA((2, chips)), DMA((2, chips)), DMA((2, chips)), DMA((2, chips)),
        ],
        compiler_params=pltpu.CompilerParams(collective_id=0, has_side_effects=True,
                                             vmem_limit_bytes=24 << 20),
        name="sketch_and_factor",
    )(*(pltpu.with_memory_space_constraint(x, pltpu.HBM) for x in (pairs, places, omega)))


def project_kernel(cols, meta_ref, basis_all_ref, basis_ref, tiles_ref, out_hbm, bases_ref, out_ref, out_sem):
    slots, n = tiles_ref.shape[0], tiles_ref.shape[1]
    groups = slots // GROUP

    def out_copy(i):
        part = pl.ds(i * GROUP, GROUP)
        return pltpu.make_async_copy(out_ref.at[part], out_hbm.at[part], out_sem.at[i])

    def step(i, carry):
        for g in range(GROUP):
            p = i * GROUP + g
            live = meta_ref[3, p].astype(jnp.float32)
            result = jnp.dot(basis_all_ref[meta_ref[0, p] // cols], tiles_ref[p],
                             preferred_element_type=jnp.float32)
            out_ref[p] = (result * live).astype(jnp.bfloat16)
        out_copy(i).start()
        return carry

    def finish(i, carry):
        out_copy(i).wait()
        return carry

    lax.fori_loop(0, groups, step, 0)
    bases_ref[...] = basis_ref[...] * math.sqrt(n)
    lax.fori_loop(0, groups, finish, 0)


def project(meta, tiles, basis, basis_all, cols):
    slots = tiles.shape[0]
    rank, n = basis_all.shape[1], basis_all.shape[2]
    return pl.pallas_call(
        functools.partial(project_kernel, cols),
        out_shape=[
            jax.ShapeDtypeStruct((slots, rank, n), jnp.bfloat16),
            jax.ShapeDtypeStruct(basis.shape, basis.dtype),
        ],
        in_specs=[pl.BlockSpec(memory_space=SMEM)] + [pl.BlockSpec(memory_space=VMEM)] * 3,
        out_specs=[pl.BlockSpec(memory_space=pl.ANY), pl.BlockSpec(memory_space=VMEM)],
        scratch_shapes=[VMEM((slots, rank, n), jnp.bfloat16), DMA((slots // GROUP,))],
        compiler_params=pltpu.CompilerParams(vmem_limit_bytes=12 << 20),
        name="project",
    )(meta, basis_all, basis, tiles)


def body(places, omega, pairs):
    rows, cols = lax.axis_size("row"), lax.axis_size("col")
    pairs = pairs.T
    tiles, basis, basis_all, meta = sketch_and_factor(pairs, places, omega, rows, cols)
    coeffs, bases = project(meta, tiles, basis, basis_all, cols)
    return (bases, coeffs)


def solution(mesh):
    in_specs = (
        P(("row", "col"), None, None),
        P(("row", "col"), None, None),
        P(("row", "col"), None),
    )
    out_specs = (P(("row", "col"), None, None), P(("row", "col"), None, None))
    return jax.shard_map(body, mesh=mesh, in_specs=in_specs, out_specs=out_specs, check_vma=False)
```

```python
import functools
import math

import jax
import jax.numpy as jnp
from jax import lax
from jax.experimental import pallas as pl
from jax.experimental.pallas import tpu as pltpu
from jax.sharding import PartitionSpec as P

soft_sq = 0.09
ridge = 0.05
MESH = pl.DeviceIdType.MESH
VMEM = pltpu.VMEM
SMEM = pltpu.SMEM
DMA = pltpu.SemaphoreType.DMA
GROUP = 32
NT = (((1,), (1,)), ((), ()))


def slot_table(cols, pairs_ref, meta_ref):
    slots = pairs_ref.shape[1]
    tgt_row = jnp.broadcast_to(pairs_ref[0:1], (slots, slots))
    src_row = jnp.broadcast_to(pairs_ref[1:2], (8, slots))
    tgt = tgt_row.T
    at_col = lax.broadcasted_iota(jnp.int32, (slots, slots), 0)
    at_row = lax.broadcasted_iota(jnp.int32, (slots, slots), 1)
    same = (tgt == tgt_row) & (tgt >= 0) & (at_col < at_row)
    last_of = (tgt >= 0) & (tgt // cols == at_row)

    def top(mask):
        best = jnp.where(mask, at_col, -1)
        rows = slots
        while rows > 8:
            rows //= 2
            best = jnp.maximum(best[:rows], best[rows:])
        for shift in (4, 2, 1):
            best = jnp.maximum(best, pltpu.roll(best, shift, 0))
        return jnp.where(best < 0, slots, best)

    live = tgt_row[0:8] >= 0
    code = jnp.where(live, tgt_row[0:8] // cols * cols + src_row % cols, 0)
    row = lax.broadcasted_iota(jnp.int32, (8, slots), 0)
    meta = jnp.where(row == 0, code, jnp.where(row == 1, top(same), top(last_of)))
    meta_ref[...] = jnp.where(row == 3, live.astype(jnp.int32), meta)


def split(x):
    hi = x.astype(jnp.bfloat16).astype(jnp.float32)
    rest = x - hi
    mid = rest.astype(jnp.bfloat16).astype(jnp.float32)
    return hi, mid, rest - mid


def target_features(spots, row8):
    n = spots.shape[1]
    coords = jnp.concatenate([spots[0:3], jnp.zeros((5, n), jnp.float32)], axis=0)
    centre = jnp.sum(coords, axis=1, keepdims=True) * (1.0 / n)
    moved = coords - centre
    norm = jnp.sum(moved * moved, axis=0, keepdims=True) + soft_sq
    feats = jnp.where(row8 == 3, norm, jnp.where(row8 == 4, 1.0, -2.0 * moved))
    hi, mid, low = split(feats)
    stack = jnp.concatenate([hi, mid, low, hi, mid, hi], axis=0)
    return stack.T.astype(jnp.bfloat16), centre


def source_features(base, scale, centre, row8):
    moved = base - centre
    norm = jnp.sum(moved * moved, axis=0, keepdims=True)
    feats = scale * jnp.where(row8 == 3, 1.0, jnp.where(row8 == 4, norm, moved))
    hi, mid, low = split(feats)
    return jnp.concatenate([hi, hi, hi, mid, mid, low], axis=0).astype(jnp.bfloat16)


def prepare_targets(tgt_ref, feat_ref, centre_ref):
    n = tgt_ref.shape[2]
    row8 = lax.broadcasted_iota(jnp.int32, (8, n), 0)

    def one(t, carry):
        feats, centre = target_features(tgt_ref[t], row8)
        feat_ref[t] = feats
        centre_ref[t] = jnp.broadcast_to(centre, (8, n))
        return carry

    lax.fori_loop(0, tgt_ref.shape[0], one, 0, unroll=4)


def prepare_sources(src_ref, base_ref, scale_ref):
    n = src_ref.shape[2]

    def one(s, carry):
        spots = src_ref[s]
        base_ref[s] = jnp.concatenate([spots[0:3], jnp.zeros((5, n), jnp.float32)], axis=0)
        weight = spots[3:4]
        scale_ref[s] = jnp.broadcast_to(1.0 / (weight * weight), (8, n))
        return carry

    lax.fori_loop(0, src_ref.shape[0], one, 0, unroll=4)


def tile_group(first, cols, meta_ref, feat_ref, centre_ref, base_ref, scale_ref, tiles_ref):
    n = feat_ref.shape[1]
    row8 = lax.broadcasted_iota(jnp.int32, (8, n), 0)
    for g in range(GROUP):
        code = meta_ref[0, first + g]
        t, s = code // cols, code % cols
        source = source_features(base_ref[s], scale_ref[s], centre_ref[t], row8)
        dist = jnp.dot(feat_ref[t], source, preferred_element_type=jnp.float32)
        tiles_ref[first + g] = lax.rsqrt(dist).astype(jnp.bfloat16)


def sketch_group(first, h, cols, meta_ref, omegas_ref, tiles_ref, running_ref):
    half = running_ref.shape[3]
    parts = []
    for g in range(GROUP):
        s = meta_ref[0, first + g] % cols
        live = meta_ref[3, first + g].astype(jnp.float32)
        part = lax.dot_general(omegas_ref[s], tiles_ref[first + g, h * half:(h + 1) * half], NT,
                               preferred_element_type=jnp.float32)
        parts.append(part * live)
    for g in range(GROUP):
        running_ref[h, first + g] = running_ref[h, meta_ref[1, first + g]] + parts[g]


def gram_of(sketch):
    return lax.dot_general(sketch, sketch, NT, precision=lax.Precision.HIGHEST,
                           preferred_element_type=jnp.float32)


def energy_of(sketch):
    return jnp.sum(jnp.sum(sketch * sketch, axis=0, keepdims=True), axis=1, keepdims=True)


def factor(sketch, gram, energy, out, at_half):
    rank, width = sketch.shape
    shift = ridge * energy / rank
    eye = (lax.broadcasted_iota(jnp.int32, (rank, rank), 0)
           == lax.broadcasted_iota(jnp.int32, (rank, rank), 1))
    mat = gram + jnp.where(eye, shift, 0.0)

    def wide(x):
        return jnp.concatenate([x] * (width // 128), axis=1)

    for b in range(0, rank, 8):
        rows = rank - b
        row_at = lax.broadcasted_iota(jnp.int32, (rows, 1), 0)
        columns = [jnp.broadcast_to(mat[:, b + j:b + j + 1], (rows, 128)) for j in range(8)]
        for k in range(8):
            inv = lax.rsqrt(columns[k][k:k + 1])
            mult = jnp.where(row_at > k, columns[k] * inv, 0.0)
            mat_row = mat[k:k + 1] * inv[:, :rank]
            sketch_row = sketch[k:k + 1] * wide(inv)
            out[b + k:b + k + 1, :] = sketch_row
            for j in range(k + 1, 8):
                columns[j] = columns[j] - mult * (columns[j][k:k + 1] * inv)
            mat = mat - mult[:, :rank] * mat_row
            sketch = sketch - wide(mult) * sketch_row
        mat, sketch = mat[8:], sketch[8:]
        if 2 * (b + 8) == rank:
            at_half()


def sketch_kernel(rows, cols, pairs_hbm, places_ref, omega_ref, tiles_ref, basis_ref, all_ref, table_ref,
                  pairs_ref, meta_ref, tgt_ref, src_ref, omegas_ref, feat_ref, centre_ref, base_ref, scale_ref,
                  running_ref, stage_ref, pair_ref, sum_ref, far_ref,
                  own_sem, row_send, row_recv, col_send, col_recv, om_send, om_recv,
                  pair_send, pair_recv, far_send, far_recv, out_send, out_recv, relay_send, relay_recv):
    row, col = lax.axis_index("row"), lax.axis_index("col")
    core, chip, chips = lax.rem(row, 2), row // 2, rows // 2
    partner = row + 1 - 2 * core
    slots = tiles_ref.shape[0]
    groups = slots // GROUP
    rank, half = running_ref.shape[2], running_ref.shape[3]
    ring, depth = chips // 2, cols // 2

    def moved(at, k, size):
        return lax.rem(at // size + k // size, 2) * size + lax.rem(lax.rem(at, size) + k % size, size)

    def moved_back(at, k, size):
        return lax.rem(at // size + k // size, 2) * size + lax.rem(lax.rem(at, size) + size - k % size, size)

    far = sorted(range(1, chips), key=lambda k: -(k // ring + min(k % ring, ring - k % ring)))
    deep = sorted(range(1, cols), key=lambda k: -(2 * (k // depth) + min(k % depth, depth - k % depth)))
    wide = [2 * k + c for k in far + [0] for c in (0, 1) if 2 * k + c]

    def row_at(k):
        return moved(chip, k // 2, ring) * 2 + lax.rem(core + k % 2, 2)

    def row_back(k):
        return moved_back(chip, k // 2, ring) * 2 + lax.rem(core + k % 2, 2)

    slot_copy = pltpu.make_async_copy(pairs_hbm, pairs_ref, own_sem.at[4])
    slot_copy.start()
    barrier = pltpu.get_barrier_semaphore()
    for k in deep:
        pl.semaphore_signal(barrier, inc=1, device_id=(row, moved(col, k, depth)), device_id_type=MESH)
    for k in wide:
        pl.semaphore_signal(barrier, inc=1, device_id=(row_at(k), col), device_id_type=MESH)
    own = [
        pltpu.make_async_copy(places_ref, tgt_ref.at[pl.ds(row, 1)], own_sem.at[0]),
        pltpu.make_async_copy(places_ref, src_ref.at[pl.ds(col, 1)], own_sem.at[1]),
        pltpu.make_async_copy(omega_ref, omegas_ref.at[pl.ds(col, 1)], own_sem.at[2]),
    ]
    for c in own:
        c.start()
    slot_copy.wait()
    slot_table(cols, pairs_ref, table_ref)
    table = pltpu.make_async_copy(table_ref, meta_ref, own_sem.at[3])
    table.start()
    for h in range(2):
        running_ref[h, slots] = jnp.zeros((rank, half), jnp.float32)
    for c in own:
        c.wait()
    pl.semaphore_wait(barrier, rows + cols - 2)

    def row_copy(k, slot):
        return pltpu.make_async_remote_copy(
            src_ref=tgt_ref.at[pl.ds(row, 1)], dst_ref=tgt_ref.at[pl.ds(slot, 1)], send_sem=row_send.at[k],
            recv_sem=row_recv.at[k], device_id=(row_at(k), col), device_id_type=MESH)

    def col_copy(k, slot):
        return pltpu.make_async_remote_copy(
            src_ref=src_ref.at[pl.ds(col, 1)], dst_ref=src_ref.at[pl.ds(slot, 1)], send_sem=col_send.at[k],
            recv_sem=col_recv.at[k], device_id=(row, moved(col, k, depth)), device_id_type=MESH)

    def om_copy(k, slot):
        return pltpu.make_async_remote_copy(
            src_ref=omegas_ref.at[pl.ds(col, 1)], dst_ref=omegas_ref.at[pl.ds(slot, 1)], send_sem=om_send.at[k],
            recv_sem=om_recv.at[k], device_id=(row, moved(col, k, depth)), device_id_type=MESH)

    def om_relay(k, slot):
        return pltpu.make_async_remote_copy(
            src_ref=omegas_ref.at[pl.ds(slot, 1)], dst_ref=omegas_ref.at[pl.ds(slot, 1)],
            send_sem=om_send.at[depth + k], recv_sem=om_recv.at[depth + k],
            device_id=(row, moved(col, depth, depth)), device_id_type=MESH)

    def hand_on(ks):
        for k in ks:
            om_copy(k, moved_back(col, k, depth)).wait_recv()
            om_relay(k, moved_back(col, k, depth)).start()

    near = sorted(range(1, depth), key=lambda k: min(k, depth - k))
    for k in deep[:cols // 2]:
        col_copy(k, col).start()
    for k in deep[cols // 2:]:
        col_copy(k, col).start()
    for k in wide:
        row_copy(k, row).start()
    om_relay(0, col).start()
    for k in near:
        om_copy(k, col).start()
    for k in wide:
        row_copy(k, row_back(k)).wait()
    prepare_targets(tgt_ref, feat_ref, centre_ref)
    for k in deep:
        col_copy(k, moved_back(col, k, depth)).wait()
    prepare_sources(src_ref, base_ref, scale_ref)
    table.wait()
    cut = len(near) // 2 + 1
    hand_on(near[:cut])

    def tile_step(i, carry):
        tile_group(i * GROUP, cols, meta_ref, feat_ref, centre_ref, base_ref, scale_ref, tiles_ref)

        @pl.when(i == 0)
        def _():
            hand_on(near[cut:-1])

        @pl.when(i == 1)
        def _():
            hand_on(near[-1:])

        return carry

    lax.fori_loop(0, groups, tile_step, 0)
    for k in near:
        om_copy(k, col).wait_send()
    for k in [0] + near:
        om_relay(k, col).wait_send()
        om_relay(k, col).wait_recv()

    def pair_copy(h, q):
        block = pl.ds(q * ring, ring)
        return pltpu.make_async_remote_copy(
            src_ref=stage_ref.at[h, block], dst_ref=pair_ref.at[h, block], send_sem=pair_send.at[h, q],
            recv_sem=pair_recv.at[h, q], device_id=(partner, col), device_id_type=MESH)

    def far_copy(h, k):
        return pltpu.make_async_remote_copy(
            src_ref=sum_ref.at[h, k], dst_ref=far_ref.at[h, k], send_sem=far_send.at[h, k],
            recv_sem=far_recv.at[h, k], device_id=(moved(chip, k, ring) * 2 + core, col), device_id_type=MESH)

    for h in range(2):
        def sketch_step(i, carry, h=h):
            sketch_group(i * GROUP, h, cols, meta_ref, omegas_ref, tiles_ref, running_ref)
            return carry

        lax.fori_loop(0, groups, sketch_step, 0)
        for q in (1, 0):
            for k in range(q * ring, (q + 1) * ring):
                stage_ref[h, k] = running_ref[h, meta_ref[2, 2 * moved(chip, k, ring) + 1 - core]]
            pair_copy(h, q).start()
        for k in range(chips):
            sum_ref[h, k] = running_ref[h, meta_ref[2, 2 * moved(chip, k, ring) + core]]
        for q in (1, 0):
            pair_copy(h, q).wait_recv()
            for k in [k for k in far if k // ring == q]:
                sum_ref[h, k] += pair_ref[h, k]
                far_copy(h, k).start()
        sum_ref[h, 0] += pair_ref[h, 0]

    totals, gram, energy = [], None, None
    for h in range(2):
        total = sum_ref[h, 0]
        for k in reversed(far):
            far_copy(h, k).wait_recv()
            total += far_ref[h, k]
        gram = gram_of(total) if h == 0 else gram + gram_of(total)
        energy = energy_of(total) if h == 0 else energy + energy_of(total)
        totals.append(total)

    part = rank // 2

    def out_copy(q, k, slot):
        block = all_ref.at[slot, pl.ds(q * part, part)]
        return pltpu.make_async_remote_copy(
            src_ref=block, dst_ref=block, send_sem=out_send.at[q, k], recv_sem=out_recv.at[q, k],
            device_id=(moved(chip, k, ring) * 2 + core, col), device_id_type=MESH)

    def relay_copy(q, k, slot):
        block = all_ref.at[slot, pl.ds(q * part, part)]
        return pltpu.make_async_remote_copy(
            src_ref=block, dst_ref=block, send_sem=relay_send.at[q, k], recv_sem=relay_recv.at[q, k],
            device_id=(partner, col), device_id_type=MESH)

    def send_part(q):
        block = pl.ds(q * part, part)
        all_ref[row, block] = basis_ref[0, block].astype(jnp.bfloat16)
        for k in far:
            out_copy(q, k, row).start()
        relay_copy(q, 0, row).start()

    factor(jnp.concatenate(totals, axis=1), gram, energy, basis_ref.at[0], lambda: send_part(0))
    send_part(1)
    for h in range(2):
        for k in far:
            far_copy(h, k).wait_send()
        for q in range(2):
            pair_copy(h, q).wait_send()
    for q in range(2):
        for k in reversed(far):
            slot = moved_back(chip, k, ring) * 2 + core
            out_copy(q, k, slot).wait_recv()
            relay_copy(q, k, slot).start()
    for q in range(2):
        for k in far:
            out_copy(q, k, row).wait_send()
        for k in [0] + far[::-1]:
            slot = moved_back(chip, k, ring) * 2 + core
            relay_copy(q, k, slot).wait_send()
            relay_copy(q, k, slot + 1 - 2 * core).wait_recv()


def sketch_and_factor(pairs, places, omega, rows, cols):
    slots = pairs.shape[1]
    rank, n = omega.shape[1], omega.shape[2]
    chips = rows // 2
    bf16, f32 = jnp.bfloat16, jnp.float32
    return pl.pallas_call(
        functools.partial(sketch_kernel, rows, cols),
        out_shape=[
            jax.ShapeDtypeStruct((slots, n, n), bf16),
            jax.ShapeDtypeStruct((1, rank, n), f32),
            jax.ShapeDtypeStruct((rows, rank, n), bf16),
            jax.ShapeDtypeStruct((8, slots), jnp.int32),
        ],
        in_specs=[pl.BlockSpec(memory_space=pltpu.HBM)] * 3,
        out_specs=[pl.BlockSpec(memory_space=VMEM)] * 4,
        scratch_shapes=[
            VMEM((2, slots), jnp.int32), SMEM((8, slots), jnp.int32),
            VMEM((rows,) + places.shape[1:], f32), VMEM((cols,) + places.shape[1:], f32),
            VMEM((cols, rank, n), bf16),
            VMEM((rows, n, 48), bf16), VMEM((rows, 8, n), f32),
            VMEM((cols, 8, n), f32), VMEM((cols, 8, n), f32),
            VMEM((2, slots + 1, rank, n // 2), f32),
            VMEM((2, chips, rank, n // 2), f32), VMEM((2, chips, rank, n // 2), f32),
            VMEM((2, chips, rank, n // 2), f32), VMEM((2, chips, rank, n // 2), f32),
            DMA((5,)), DMA((rows,)), DMA((rows,)), DMA((cols,)), DMA((cols,)), DMA((cols,)), DMA((cols,)),
            DMA((2, 2)), DMA((2, 2)), DMA((2, chips)), DMA((2, chips)),
            DMA((2, chips)), DMA((2, chips)), DMA((2, chips)), DMA((2, chips)),
        ],
        compiler_params=pltpu.CompilerParams(collective_id=0, has_side_effects=True,
                                             vmem_limit_bytes=24 << 20),
        name="sketch_and_factor",
    )(*(pltpu.with_memory_space_constraint(x, pltpu.HBM) for x in (pairs, places, omega)))


def project_kernel(cols, meta_ref, basis_all_ref, basis_ref, tiles_ref, out_hbm, bases_ref, out_ref, out_sem):
    slots, n = tiles_ref.shape[0], tiles_ref.shape[1]
    groups = slots // GROUP

    def out_copy(i):
        part = pl.ds(i * GROUP, GROUP)
        return pltpu.make_async_copy(out_ref.at[part], out_hbm.at[part], out_sem.at[i])

    def step(i, carry):
        for g in range(GROUP):
            p = i * GROUP + g
            live = meta_ref[3, p].astype(jnp.float32)
            result = jnp.dot(basis_all_ref[meta_ref[0, p] // cols], tiles_ref[p],
                             preferred_element_type=jnp.float32)
            out_ref[p] = (result * live).astype(jnp.bfloat16)
        out_copy(i).start()
        return carry

    def finish(i, carry):
        out_copy(i).wait()
        return carry

    lax.fori_loop(0, groups, step, 0)
    bases_ref[...] = basis_ref[...] * math.sqrt(n)
    lax.fori_loop(0, groups, finish, 0)


def project(meta, tiles, basis, basis_all, cols):
    slots = tiles.shape[0]
    rank, n = basis_all.shape[1], basis_all.shape[2]
    return pl.pallas_call(
        functools.partial(project_kernel, cols),
        out_shape=[
            jax.ShapeDtypeStruct((slots, rank, n), jnp.bfloat16),
            jax.ShapeDtypeStruct(basis.shape, basis.dtype),
        ],
        in_specs=[pl.BlockSpec(memory_space=SMEM)] + [pl.BlockSpec(memory_space=VMEM)] * 3,
        out_specs=[pl.BlockSpec(memory_space=pl.ANY), pl.BlockSpec(memory_space=VMEM)],
        scratch_shapes=[VMEM((slots, rank, n), jnp.bfloat16), DMA((slots // GROUP,))],
        compiler_params=pltpu.CompilerParams(vmem_limit_bytes=12 << 20),
        name="project",
    )(meta, basis_all, basis, tiles)


def body(places, omega, pairs):
    rows, cols = lax.axis_size("row"), lax.axis_size("col")
    pairs = pairs.T
    tiles, basis, basis_all, meta = sketch_and_factor(pairs, places, omega, rows, cols)
    coeffs, bases = project(meta, tiles, basis, basis_all, cols)
    return (bases, coeffs)


def solution(mesh):
    in_specs = (
        P(("row", "col"), None, None),
        P(("row", "col"), None, None),
        P(("row", "col"), None),
    )
    out_specs = (P(("row", "col"), None, None), P(("row", "col"), None, None))
    return jax.shard_map(body, mesh=mesh, in_specs=in_specs, out_specs=out_specs, check_vma=False)
```

```python
import functools
import math

import jax
import jax.numpy as jnp
from jax import lax
from jax.experimental import pallas as pl
from jax.experimental.pallas import tpu as pltpu
from jax.sharding import PartitionSpec as P

soft_sq = 0.09
ridge = 0.05
MESH = pl.DeviceIdType.MESH
VMEM = pltpu.VMEM
SMEM = pltpu.SMEM
DMA = pltpu.SemaphoreType.DMA
GROUP = 32
NT = (((1,), (1,)), ((), ()))


def slot_table(cols, pairs_ref, meta_ref):
    slots = pairs_ref.shape[1]
    tgt_row = jnp.broadcast_to(pairs_ref[0:1], (slots, slots))
    src_row = jnp.broadcast_to(pairs_ref[1:2], (8, slots))
    tgt = tgt_row.T
    at_col = lax.broadcasted_iota(jnp.int32, (slots, slots), 0)
    at_row = lax.broadcasted_iota(jnp.int32, (slots, slots), 1)
    same = (tgt == tgt_row) & (tgt >= 0) & (at_col < at_row)
    last_of = (tgt >= 0) & (tgt // cols == at_row)

    def top(mask):
        best = jnp.where(mask, at_col, -1)
        rows = slots
        while rows > 8:
            rows //= 2
            best = jnp.maximum(best[:rows], best[rows:])
        for shift in (4, 2, 1):
            best = jnp.maximum(best, pltpu.roll(best, shift, 0))
        return jnp.where(best < 0, slots, best)

    live = tgt_row[0:8] >= 0
    code = jnp.where(live, tgt_row[0:8] // cols * cols + src_row % cols, 0)
    row = lax.broadcasted_iota(jnp.int32, (8, slots), 0)
    meta = jnp.where(row == 0, code, jnp.where(row == 1, top(same), top(last_of)))
    meta_ref[...] = jnp.where(row == 3, live.astype(jnp.int32), meta)


def split(x):
    hi = x.astype(jnp.bfloat16).astype(jnp.float32)
    rest = x - hi
    mid = rest.astype(jnp.bfloat16).astype(jnp.float32)
    return hi, mid, rest - mid


def coords_of(spots):
    return jnp.concatenate([spots[0:3], jnp.zeros((5, spots.shape[1]), jnp.float32)], axis=0)


def streamed(base, scale, row8):
    centre = jnp.sum(base, axis=1, keepdims=True) * (1.0 / base.shape[1])
    moved = base - centre
    norm = jnp.sum(moved * moved, axis=0, keepdims=True) + soft_sq
    feats = scale * jnp.where(row8 == 3, norm, jnp.where(row8 == 4, 1.0, -2.0 * moved))
    hi, mid, low = split(feats)
    stack = jnp.concatenate([hi, mid, low, hi, mid, hi], axis=0)
    return stack.T.astype(jnp.bfloat16), jnp.broadcast_to(centre, base.shape)


def held(base, scale, centre, row8):
    moved = base - centre
    norm = jnp.sum(moved * moved, axis=0, keepdims=True)
    feats = scale * jnp.where(row8 == 3, 1.0, jnp.where(row8 == 4, norm, moved))
    hi, mid, low = split(feats)
    return jnp.concatenate([hi, hi, hi, mid, mid, low], axis=0).astype(jnp.bfloat16)


def prepare_targets(tgt_ref, base_ref, feat_ref, centre_ref):
    n = tgt_ref.shape[2]
    row8 = lax.broadcasted_iota(jnp.int32, (8, n), 0)

    def one(t, carry):
        base = coords_of(tgt_ref[t])
        base_ref[t] = base
        feat_ref[t], centre_ref[t] = streamed(base, 1.0, row8)
        return carry

    lax.fori_loop(0, tgt_ref.shape[0], one, 0, unroll=4)


def prepare_sources(src_ref, base_ref, scale_ref, feat_ref, centre_ref):
    n = src_ref.shape[2]
    row8 = lax.broadcasted_iota(jnp.int32, (8, n), 0)

    def one(s, carry):
        spots = src_ref[s]
        base = coords_of(spots)
        weight = spots[3:4]
        scale = jnp.broadcast_to(1.0 / (weight * weight), (8, n))
        base_ref[s], scale_ref[s] = base, scale
        feat_ref[s], centre_ref[s] = streamed(base, scale, row8)
        return carry

    lax.fori_loop(0, src_ref.shape[0], one, 0, unroll=4)


def turned_group(first, cols, meta_ref, tgt_base, src_feat, src_centre, turned_ref):
    n = src_feat.shape[1]
    row8 = lax.broadcasted_iota(jnp.int32, (8, n), 0)
    for g in range(GROUP):
        code = meta_ref[0, first + g]
        t, s = code // cols, code % cols
        target = held(tgt_base[t], 1.0, src_centre[s], row8)
        dist = jnp.dot(src_feat[s], target, preferred_element_type=jnp.float32)
        turned_ref[first + g] = lax.rsqrt(dist).astype(jnp.bfloat16)


def tile_group(first, cols, meta_ref, src_base, src_scale, tgt_feat, tgt_centre, tiles_ref):
    n = tgt_feat.shape[1]
    row8 = lax.broadcasted_iota(jnp.int32, (8, n), 0)
    for g in range(GROUP):
        code = meta_ref[0, first + g]
        t, s = code // cols, code % cols
        source = held(src_base[s], src_scale[s], tgt_centre[t], row8)
        dist = jnp.dot(tgt_feat[t], source, preferred_element_type=jnp.float32)
        tiles_ref[first + g] = lax.rsqrt(dist).astype(jnp.bfloat16)


def sketch_group(first, h, cols, meta_ref, omegas_ref, turned_ref, running_ref):
    half = running_ref.shape[3]
    parts = []
    for g in range(GROUP):
        s = meta_ref[0, first + g] % cols
        live = meta_ref[3, first + g].astype(jnp.float32)
        part = jnp.dot(omegas_ref[s], turned_ref[first + g, :, h * half:(h + 1) * half],
                       preferred_element_type=jnp.float32)
        parts.append(part * live)
    for g in range(GROUP):
        running_ref[h, first + g] = running_ref[h, meta_ref[1, first + g]] + parts[g]


def gram_of(sketch):
    return lax.dot_general(sketch, sketch, NT, precision=lax.Precision.HIGHEST,
                           preferred_element_type=jnp.float32)


def energy_of(sketch):
    return jnp.sum(jnp.sum(sketch * sketch, axis=0, keepdims=True), axis=1, keepdims=True)


def factor(sketch, gram, energy, out, at_half):
    rank, width = sketch.shape
    shift = ridge * energy / rank
    eye = (lax.broadcasted_iota(jnp.int32, (rank, rank), 0)
           == lax.broadcasted_iota(jnp.int32, (rank, rank), 1))
    mat = gram + jnp.where(eye, shift, 0.0)

    def wide(x):
        return jnp.concatenate([x] * (width // 128), axis=1)

    for b in range(0, rank, 8):
        rows = rank - b
        row_at = lax.broadcasted_iota(jnp.int32, (rows, 1), 0)
        columns = [jnp.broadcast_to(mat[:, b + j:b + j + 1], (rows, 128)) for j in range(8)]
        for k in range(8):
            inv = lax.rsqrt(columns[k][k:k + 1])
            mult = jnp.where(row_at > k, columns[k] * inv, 0.0)
            mat_row = mat[k:k + 1] * inv[:, :rank]
            sketch_row = sketch[k:k + 1] * wide(inv)
            out[b + k:b + k + 1, :] = sketch_row
            for j in range(k + 1, 8):
                columns[j] = columns[j] - mult * (columns[j][k:k + 1] * inv)
            mat = mat - mult[:, :rank] * mat_row
            sketch = sketch - wide(mult) * sketch_row
        mat, sketch = mat[8:], sketch[8:]
        if 2 * (b + 8) == rank:
            at_half()


def sketch_kernel(rows, cols, pairs_hbm, places_ref, omega_ref, tiles_ref, basis_ref, all_ref, table_ref,
                  pairs_ref, meta_ref, tgt_ref, src_ref, omegas_ref, tgt_base, tgt_feat, tgt_centre,
                  src_base, src_scale, src_feat, src_centre, turned_ref, running_ref, stage_ref, pair_ref, sum_ref, far_ref,
                  own_sem, row_send, row_recv, col_send, col_recv, om_send, om_recv,
                  pair_send, pair_recv, far_send, far_recv, out_send, out_recv, relay_send, relay_recv):
    row, col = lax.axis_index("row"), lax.axis_index("col")
    core, chip, chips = lax.rem(row, 2), row // 2, rows // 2
    partner = row + 1 - 2 * core
    slots = tiles_ref.shape[0]
    groups = slots // GROUP
    rank, half = running_ref.shape[2], running_ref.shape[3]
    ring, depth = chips // 2, cols // 2

    def moved(at, k, size):
        return lax.rem(at // size + k // size, 2) * size + lax.rem(lax.rem(at, size) + k % size, size)

    def moved_back(at, k, size):
        return lax.rem(at // size + k // size, 2) * size + lax.rem(lax.rem(at, size) + size - k % size, size)

    far = sorted(range(1, chips), key=lambda k: -(k // ring + min(k % ring, ring - k % ring)))
    deep = sorted(range(1, cols), key=lambda k: -(2 * (k // depth) + min(k % depth, depth - k % depth)))
    wide = [2 * k + c for k in far + [0] for c in (0, 1) if 2 * k + c]

    def row_at(k):
        return moved(chip, k // 2, ring) * 2 + lax.rem(core + k % 2, 2)

    def row_back(k):
        return moved_back(chip, k // 2, ring) * 2 + lax.rem(core + k % 2, 2)

    slot_copy = pltpu.make_async_copy(pairs_hbm, pairs_ref, own_sem.at[4])
    slot_copy.start()
    barrier = pltpu.get_barrier_semaphore()
    for k in deep:
        pl.semaphore_signal(barrier, inc=1, device_id=(row, moved(col, k, depth)), device_id_type=MESH)
    for k in wide:
        pl.semaphore_signal(barrier, inc=1, device_id=(row_at(k), col), device_id_type=MESH)
    own = [
        pltpu.make_async_copy(places_ref, tgt_ref.at[pl.ds(row, 1)], own_sem.at[0]),
        pltpu.make_async_copy(places_ref, src_ref.at[pl.ds(col, 1)], own_sem.at[1]),
        pltpu.make_async_copy(omega_ref, omegas_ref.at[pl.ds(col, 1)], own_sem.at[2]),
    ]
    for c in own:
        c.start()
    slot_copy.wait()
    slot_table(cols, pairs_ref, table_ref)
    table = pltpu.make_async_copy(table_ref, meta_ref, own_sem.at[3])
    table.start()
    for h in range(2):
        running_ref[h, slots] = jnp.zeros((rank, half), jnp.float32)
    for c in own:
        c.wait()
    pl.semaphore_wait(barrier, rows + cols - 2)

    def row_copy(k, slot):
        return pltpu.make_async_remote_copy(
            src_ref=tgt_ref.at[pl.ds(row, 1)], dst_ref=tgt_ref.at[pl.ds(slot, 1)], send_sem=row_send.at[k],
            recv_sem=row_recv.at[k], device_id=(row_at(k), col), device_id_type=MESH)

    def col_copy(k, slot):
        return pltpu.make_async_remote_copy(
            src_ref=src_ref.at[pl.ds(col, 1)], dst_ref=src_ref.at[pl.ds(slot, 1)], send_sem=col_send.at[k],
            recv_sem=col_recv.at[k], device_id=(row, moved(col, k, depth)), device_id_type=MESH)

    def om_copy(k, slot):
        return pltpu.make_async_remote_copy(
            src_ref=omegas_ref.at[pl.ds(col, 1)], dst_ref=omegas_ref.at[pl.ds(slot, 1)], send_sem=om_send.at[k],
            recv_sem=om_recv.at[k], device_id=(row, moved(col, k, depth)), device_id_type=MESH)

    def om_relay(k, slot):
        return pltpu.make_async_remote_copy(
            src_ref=omegas_ref.at[pl.ds(slot, 1)], dst_ref=omegas_ref.at[pl.ds(slot, 1)],
            send_sem=om_send.at[depth + k], recv_sem=om_recv.at[depth + k],
            device_id=(row, moved(col, depth, depth)), device_id_type=MESH)

    def hand_on(ks):
        for k in ks:
            om_copy(k, moved_back(col, k, depth)).wait_recv()
            om_relay(k, moved_back(col, k, depth)).start()

    near = sorted(range(1, depth), key=lambda k: min(k, depth - k))
    for k in deep[:cols // 2]:
        col_copy(k, col).start()
    for k in deep[cols // 2:]:
        col_copy(k, col).start()
    for k in wide:
        row_copy(k, row).start()
    om_relay(0, col).start()
    for k in near:
        om_copy(k, col).start()
    for k in wide:
        row_copy(k, row_back(k)).wait()
    prepare_targets(tgt_ref, tgt_base, tgt_feat, tgt_centre)
    for k in deep:
        col_copy(k, moved_back(col, k, depth)).wait()
    prepare_sources(src_ref, src_base, src_scale, src_feat, src_centre)
    table.wait()
    cut = len(near) // 2 + 1
    hand_on(near[:cut])

    def turned_step(i, carry):
        turned_group(i * GROUP, cols, meta_ref, tgt_base, src_feat, src_centre, turned_ref)

        @pl.when(i == 0)
        def _():
            hand_on(near[cut:-1])

        @pl.when(i == 1)
        def _():
            hand_on(near[-1:])

        return carry

    lax.fori_loop(0, groups, turned_step, 0)
    for k in near:
        om_copy(k, col).wait_send()
    for k in [0] + near:
        om_relay(k, col).wait_send()
        om_relay(k, col).wait_recv()

    def pair_copy(h, q):
        block = pl.ds(q * ring, ring)
        return pltpu.make_async_remote_copy(
            src_ref=stage_ref.at[h, block], dst_ref=pair_ref.at[h, block], send_sem=pair_send.at[h, q],
            recv_sem=pair_recv.at[h, q], device_id=(partner, col), device_id_type=MESH)

    def far_copy(h, k):
        return pltpu.make_async_remote_copy(
            src_ref=sum_ref.at[h, k], dst_ref=far_ref.at[h, k], send_sem=far_send.at[h, k],
            recv_sem=far_recv.at[h, k], device_id=(moved(chip, k, ring) * 2 + core, col), device_id_type=MESH)

    def swap(h):
        for q in (1, 0):
            for k in range(q * ring, (q + 1) * ring):
                stage_ref[h, k] = running_ref[h, meta_ref[2, 2 * moved(chip, k, ring) + 1 - core]]
            pair_copy(h, q).start()
        for k in range(chips):
            sum_ref[h, k] = running_ref[h, meta_ref[2, 2 * moved(chip, k, ring) + core]]

    def send_sums(h):
        for q in (1, 0):
            pair_copy(h, q).wait_recv()
            for k in [k for k in far if k // ring == q]:
                sum_ref[h, k] += pair_ref[h, k]
                far_copy(h, k).start()
        sum_ref[h, 0] += pair_ref[h, 0]

    def first_half(i, carry):
        sketch_group(i * GROUP, 0, cols, meta_ref, omegas_ref, turned_ref, running_ref)
        return carry

    def second_half(i, carry):
        @pl.when(i == groups // 2)
        def _():
            send_sums(0)

        sketch_group(i * GROUP, 1, cols, meta_ref, omegas_ref, turned_ref, running_ref)
        return carry

    lax.fori_loop(0, groups, first_half, 0)
    swap(0)
    lax.fori_loop(0, groups, second_half, 0)
    swap(1)

    def tile_step(i, carry):
        @pl.when(i == 1)
        def _():
            send_sums(1)

        tile_group(i * GROUP, cols, meta_ref, src_base, src_scale, tgt_feat, tgt_centre, tiles_ref)
        return carry

    lax.fori_loop(0, groups, tile_step, 0)

    totals, gram, energy = [], None, None
    for h in range(2):
        total = sum_ref[h, 0]
        for k in reversed(far):
            far_copy(h, k).wait_recv()
            total += far_ref[h, k]
        gram = gram_of(total) if h == 0 else gram + gram_of(total)
        energy = energy_of(total) if h == 0 else energy + energy_of(total)
        totals.append(total)

    part = rank // 2

    def out_copy(q, k, slot):
        block = all_ref.at[slot, pl.ds(q * part, part)]
        return pltpu.make_async_remote_copy(
            src_ref=block, dst_ref=block, send_sem=out_send.at[q, k], recv_sem=out_recv.at[q, k],
            device_id=(moved(chip, k, ring) * 2 + core, col), device_id_type=MESH)

    def relay_copy(q, k, slot):
        block = all_ref.at[slot, pl.ds(q * part, part)]
        return pltpu.make_async_remote_copy(
            src_ref=block, dst_ref=block, send_sem=relay_send.at[q, k], recv_sem=relay_recv.at[q, k],
            device_id=(partner, col), device_id_type=MESH)

    def send_part(q):
        block = pl.ds(q * part, part)
        all_ref[row, block] = basis_ref[0, block].astype(jnp.bfloat16)
        for k in far:
            out_copy(q, k, row).start()
        relay_copy(q, 0, row).start()

    factor(jnp.concatenate(totals, axis=1), gram, energy, basis_ref.at[0], lambda: send_part(0))
    send_part(1)
    for h in range(2):
        for k in far:
            far_copy(h, k).wait_send()
        for q in range(2):
            pair_copy(h, q).wait_send()
    for q in range(2):
        for k in reversed(far):
            slot = moved_back(chip, k, ring) * 2 + core
            out_copy(q, k, slot).wait_recv()
            relay_copy(q, k, slot).start()
    for q in range(2):
        for k in far:
            out_copy(q, k, row).wait_send()
        for k in [0] + far[::-1]:
            slot = moved_back(chip, k, ring) * 2 + core
            relay_copy(q, k, slot).wait_send()
            relay_copy(q, k, slot + 1 - 2 * core).wait_recv()


def sketch_and_factor(pairs, places, omega, rows, cols):
    slots = pairs.shape[1]
    rank, n = omega.shape[1], omega.shape[2]
    chips = rows // 2
    bf16, f32 = jnp.bfloat16, jnp.float32
    return pl.pallas_call(
        functools.partial(sketch_kernel, rows, cols),
        out_shape=[
            jax.ShapeDtypeStruct((slots, n, n), bf16),
            jax.ShapeDtypeStruct((1, rank, n), f32),
            jax.ShapeDtypeStruct((rows, rank, n), bf16),
            jax.ShapeDtypeStruct((8, slots), jnp.int32),
        ],
        in_specs=[pl.BlockSpec(memory_space=pltpu.HBM)] * 3,
        out_specs=[pl.BlockSpec(memory_space=VMEM)] * 4,
        scratch_shapes=[
            VMEM((2, slots), jnp.int32), SMEM((8, slots), jnp.int32),
            VMEM((rows,) + places.shape[1:], f32), VMEM((cols,) + places.shape[1:], f32),
            VMEM((cols, rank, n), bf16),
            VMEM((rows, 8, n), f32), VMEM((rows, n, 48), bf16), VMEM((rows, 8, n), f32),
            VMEM((cols, 8, n), f32), VMEM((cols, 8, n), f32), VMEM((cols, n, 48), bf16), VMEM((cols, 8, n), f32),
            VMEM((slots, n, n), bf16),
            VMEM((2, slots + 1, rank, n // 2), f32),
            VMEM((2, chips, rank, n // 2), f32), VMEM((2, chips, rank, n // 2), f32),
            VMEM((2, chips, rank, n // 2), f32), VMEM((2, chips, rank, n // 2), f32),
            DMA((5,)), DMA((rows,)), DMA((rows,)), DMA((cols,)), DMA((cols,)), DMA((cols,)), DMA((cols,)),
            DMA((2, 2)), DMA((2, 2)), DMA((2, chips)), DMA((2, chips)),
            DMA((2, chips)), DMA((2, chips)), DMA((2, chips)), DMA((2, chips)),
        ],
        compiler_params=pltpu.CompilerParams(collective_id=0, has_side_effects=True,
                                             vmem_limit_bytes=36 << 20),
        name="sketch_and_factor",
    )(*(pltpu.with_memory_space_constraint(x, pltpu.HBM) for x in (pairs, places, omega)))


def project_kernel(cols, meta_ref, basis_all_ref, basis_ref, tiles_ref, out_hbm, bases_ref, out_ref, out_sem):
    slots, n = tiles_ref.shape[0], tiles_ref.shape[1]
    groups = slots // GROUP

    def out_copy(i):
        part = pl.ds(i * GROUP, GROUP)
        return pltpu.make_async_copy(out_ref.at[part], out_hbm.at[part], out_sem.at[i])

    def step(i, carry):
        for g in range(GROUP):
            p = i * GROUP + g
            live = meta_ref[3, p].astype(jnp.float32)
            result = jnp.dot(basis_all_ref[meta_ref[0, p] // cols], tiles_ref[p],
                             preferred_element_type=jnp.float32)
            out_ref[p] = (result * live).astype(jnp.bfloat16)
        out_copy(i).start()
        return carry

    def finish(i, carry):
        out_copy(i).wait()
        return carry

    lax.fori_loop(0, groups, step, 0)
    bases_ref[...] = basis_ref[...] * math.sqrt(n)
    lax.fori_loop(0, groups, finish, 0)


def project(meta, tiles, basis, basis_all, cols):
    slots = tiles.shape[0]
    rank, n = basis_all.shape[1], basis_all.shape[2]
    return pl.pallas_call(
        functools.partial(project_kernel, cols),
        out_shape=[
            jax.ShapeDtypeStruct((slots, rank, n), jnp.bfloat16),
            jax.ShapeDtypeStruct(basis.shape, basis.dtype),
        ],
        in_specs=[pl.BlockSpec(memory_space=SMEM)] + [pl.BlockSpec(memory_space=VMEM)] * 3,
        out_specs=[pl.BlockSpec(memory_space=pl.ANY), pl.BlockSpec(memory_space=VMEM)],
        scratch_shapes=[VMEM((slots, rank, n), jnp.bfloat16), DMA((slots // GROUP,))],
        compiler_params=pltpu.CompilerParams(vmem_limit_bytes=12 << 20),
        name="project",
    )(meta, basis_all, basis, tiles)


def body(places, omega, pairs):
    rows, cols = lax.axis_size("row"), lax.axis_size("col")
    pairs = pairs.T
    tiles, basis, basis_all, meta = sketch_and_factor(pairs, places, omega, rows, cols)
    coeffs, bases = project(meta, tiles, basis, basis_all, cols)
    return (bases, coeffs)


def solution(mesh):
    in_specs = (
        P(("row", "col"), None, None),
        P(("row", "col"), None, None),
        P(("row", "col"), None),
    )
    out_specs = (P(("row", "col"), None, None), P(("row", "col"), None, None))
    return jax.shard_map(body, mesh=mesh, in_specs=in_specs, out_specs=out_specs, check_vma=False)
```

```python
import functools
import math

import jax
import jax.numpy as jnp
from jax import lax
from jax.experimental import pallas as pl
from jax.experimental.pallas import tpu as pltpu
from jax.sharding import PartitionSpec as P

soft_sq = 0.09
ridge = 0.05
MESH = pl.DeviceIdType.MESH
VMEM = pltpu.VMEM
SMEM = pltpu.SMEM
DMA = pltpu.SemaphoreType.DMA
GROUP = 32
LONG = 64
PIECE = 16
NT = (((1,), (1,)), ((), ()))


def slot_table(cols, pairs_ref, meta_ref):
    slots = pairs_ref.shape[1]
    tgt_row = jnp.broadcast_to(pairs_ref[0:1], (slots, slots))
    src_row = jnp.broadcast_to(pairs_ref[1:2], (8, slots))
    tgt = tgt_row.T
    at_col = lax.broadcasted_iota(jnp.int32, (slots, slots), 0)
    at_row = lax.broadcasted_iota(jnp.int32, (slots, slots), 1)
    same = (tgt == tgt_row) & (tgt >= 0) & (at_col < at_row)
    last_of = (tgt >= 0) & (tgt // cols == at_row)

    def top(mask):
        best = jnp.where(mask, at_col, -1)
        rows = slots
        while rows > 8:
            rows //= 2
            best = jnp.maximum(best[:rows], best[rows:])
        for shift in (4, 2, 1):
            best = jnp.maximum(best, pltpu.roll(best, shift, 0))
        return jnp.where(best < 0, slots, best)

    live = tgt_row[0:8] >= 0
    code = jnp.where(live, tgt_row[0:8] // cols * cols + src_row % cols, 0)
    row = lax.broadcasted_iota(jnp.int32, (8, slots), 0)
    meta = jnp.where(row == 0, code, jnp.where(row == 1, top(same), top(last_of)))
    meta_ref[...] = jnp.where(row == 3, live.astype(jnp.int32), meta)


def split(x):
    hi = x.astype(jnp.bfloat16).astype(jnp.float32)
    rest = x - hi
    mid = rest.astype(jnp.bfloat16).astype(jnp.float32)
    return hi, mid, rest - mid


def coords_of(spots):
    return jnp.concatenate([spots[0:3], jnp.zeros((5, spots.shape[1]), jnp.float32)], axis=0)


def streamed(base, scale, row8):
    centre = jnp.sum(base, axis=1, keepdims=True) * (1.0 / base.shape[1])
    moved = base - centre
    norm = jnp.sum(moved * moved, axis=0, keepdims=True) + soft_sq
    feats = scale * jnp.where(row8 == 3, norm, jnp.where(row8 == 4, 1.0, -2.0 * moved))
    hi, mid, low = split(feats)
    stack = jnp.concatenate([hi, mid, low, hi, mid, hi], axis=0)
    return stack.T.astype(jnp.bfloat16), jnp.broadcast_to(centre, base.shape)


def held(base, scale, centre, row8):
    moved = base - centre
    norm = jnp.sum(moved * moved, axis=0, keepdims=True)
    feats = scale * jnp.where(row8 == 3, 1.0, jnp.where(row8 == 4, norm, moved))
    hi, mid, low = split(feats)
    return jnp.concatenate([hi, hi, hi, mid, mid, low], axis=0).astype(jnp.bfloat16)


def prepare_targets(tgt_ref, base_ref, feat_ref, centre_ref):
    n = tgt_ref.shape[2]
    row8 = lax.broadcasted_iota(jnp.int32, (8, n), 0)

    def one(t, carry):
        base = coords_of(tgt_ref[t])
        base_ref[t] = base
        feat_ref[t], centre_ref[t] = streamed(base, 1.0, row8)
        return carry

    lax.fori_loop(0, tgt_ref.shape[0], one, 0, unroll=4)


def prepare_sources(src_ref, base_ref, scale_ref, feat_ref, centre_ref):
    n = src_ref.shape[2]
    row8 = lax.broadcasted_iota(jnp.int32, (8, n), 0)

    def one(s, carry):
        spots = src_ref[s]
        base = coords_of(spots)
        weight = spots[3:4]
        scale = jnp.broadcast_to(1.0 / (weight * weight), (8, n))
        base_ref[s], scale_ref[s] = base, scale
        feat_ref[s], centre_ref[s] = streamed(base, scale, row8)
        return carry

    lax.fori_loop(0, src_ref.shape[0], one, 0, unroll=4)


def turned_group(first, cols, meta_ref, tgt_base, src_feat, src_centre, turned_ref):
    n = src_feat.shape[1]
    row8 = lax.broadcasted_iota(jnp.int32, (8, n), 0)
    for g in range(GROUP):
        code = meta_ref[0, first + g]
        t, s = code // cols, code % cols
        target = held(tgt_base[t], 1.0, src_centre[s], row8)
        dist = jnp.dot(src_feat[s], target, preferred_element_type=jnp.float32)
        turned_ref[first + g] = lax.rsqrt(dist).astype(jnp.bfloat16)


def tile_group(first, cols, meta_ref, src_base, src_scale, tgt_feat, tgt_centre, tiles_ref):
    n = tgt_feat.shape[1]
    row8 = lax.broadcasted_iota(jnp.int32, (8, n), 0)
    for g in range(GROUP):
        code = meta_ref[0, first + g]
        t, s = code // cols, code % cols
        source = held(src_base[s], src_scale[s], tgt_centre[t], row8)
        dist = jnp.dot(tgt_feat[t], source, preferred_element_type=jnp.float32)
        tiles_ref[first + g] = lax.rsqrt(dist).astype(jnp.bfloat16)


def sketch_group(first, h, cols, meta_ref, omegas_ref, turned_ref, running_ref):
    half = running_ref.shape[3]
    parts = []
    for g in range(GROUP):
        s = meta_ref[0, first + g] % cols
        live = meta_ref[3, first + g].astype(jnp.float32)
        part = jnp.dot(omegas_ref[s], turned_ref[first + g, :, h * half:(h + 1) * half],
                       preferred_element_type=jnp.float32)
        parts.append(part * live)
    for g in range(GROUP):
        running_ref[h, first + g] = running_ref[h, meta_ref[1, first + g]] + parts[g]


def gram_of(sketch):
    return lax.dot_general(sketch, sketch, NT, precision=lax.Precision.HIGHEST,
                           preferred_element_type=jnp.float32)


def energy_of(sketch):
    return jnp.sum(jnp.sum(sketch * sketch, axis=0, keepdims=True), axis=1, keepdims=True)


def factor(sketch, gram, energy, out, at_half):
    rank, width = sketch.shape
    shift = ridge * energy / rank
    eye = (lax.broadcasted_iota(jnp.int32, (rank, rank), 0)
           == lax.broadcasted_iota(jnp.int32, (rank, rank), 1))
    mat = gram + jnp.where(eye, shift, 0.0)

    def wide(x):
        return jnp.concatenate([x] * (width // 128), axis=1)

    for b in range(0, rank, 8):
        rows = rank - b
        row_at = lax.broadcasted_iota(jnp.int32, (rows, 1), 0)
        columns = [jnp.broadcast_to(mat[:, b + j:b + j + 1], (rows, 128)) for j in range(8)]
        for k in range(8):
            inv = lax.rsqrt(columns[k][k:k + 1])
            mult = jnp.where(row_at > k, columns[k] * inv, 0.0)
            mat_row = mat[k:k + 1] * inv[:, :rank]
            sketch_row = sketch[k:k + 1] * wide(inv)
            out[b + k:b + k + 1, :] = sketch_row
            for j in range(k + 1, 8):
                columns[j] = columns[j] - mult * (columns[j][k:k + 1] * inv)
            mat = mat - mult[:, :rank] * mat_row
            sketch = sketch - wide(mult) * sketch_row
        mat, sketch = mat[8:], sketch[8:]
        if 2 * (b + 8) == rank:
            at_half()


def sketch_kernel(rows, cols, pairs_hbm, places_ref, omega_ref, tiles_ref, basis_ref, all_ref, table_ref,
                  pairs_ref, meta_ref, tgt_ref, src_ref, omegas_ref, tgt_base, tgt_feat, tgt_centre,
                  src_base, src_scale, src_feat, src_centre, turned_ref, running_ref, stage_ref, pair_ref, sum_ref, far_ref,
                  own_sem, row_send, row_recv, col_send, col_recv, om_send, om_recv,
                  pair_send, pair_recv, far_send, far_recv, out_send, out_recv, relay_send, relay_recv):
    row, col = lax.axis_index("row"), lax.axis_index("col")
    core, chip, chips = lax.rem(row, 2), row // 2, rows // 2
    partner = row + 1 - 2 * core
    slots = tiles_ref.shape[0]
    groups = slots // GROUP
    rank, half = running_ref.shape[2], running_ref.shape[3]
    ring, depth = chips // 2, cols // 2

    def moved(at, k, size):
        return lax.rem(at // size + k // size, 2) * size + lax.rem(lax.rem(at, size) + k % size, size)

    def moved_back(at, k, size):
        return lax.rem(at // size + k // size, 2) * size + lax.rem(lax.rem(at, size) + size - k % size, size)

    far = sorted(range(1, chips), key=lambda k: -(k // ring + min(k % ring, ring - k % ring)))
    deep = sorted(range(1, cols), key=lambda k: -(2 * (k // depth) + min(k % depth, depth - k % depth)))
    wide = [2 * k + c for k in far + [0] for c in (0, 1) if 2 * k + c]

    def row_at(k):
        return moved(chip, k // 2, ring) * 2 + lax.rem(core + k % 2, 2)

    def row_back(k):
        return moved_back(chip, k // 2, ring) * 2 + lax.rem(core + k % 2, 2)

    slot_copy = pltpu.make_async_copy(pairs_hbm, pairs_ref, own_sem.at[4])
    slot_copy.start()
    barrier = pltpu.get_barrier_semaphore()
    for k in deep:
        pl.semaphore_signal(barrier, inc=1, device_id=(row, moved(col, k, depth)), device_id_type=MESH)
    for k in wide:
        pl.semaphore_signal(barrier, inc=1, device_id=(row_at(k), col), device_id_type=MESH)
    own = [
        pltpu.make_async_copy(places_ref, tgt_ref.at[pl.ds(row, 1)], own_sem.at[0]),
        pltpu.make_async_copy(places_ref, src_ref.at[pl.ds(col, 1)], own_sem.at[1]),
        pltpu.make_async_copy(omega_ref, omegas_ref.at[pl.ds(col, 1)], own_sem.at[2]),
    ]
    for c in own:
        c.start()
    slot_copy.wait()
    slot_table(cols, pairs_ref, table_ref)
    table = pltpu.make_async_copy(table_ref, meta_ref, own_sem.at[3])
    table.start()
    for h in range(2):
        running_ref[h, slots] = jnp.zeros((rank, half), jnp.float32)
    for c in own:
        c.wait()
    pl.semaphore_wait(barrier, rows + cols - 2)

    def row_copy(k, slot):
        return pltpu.make_async_remote_copy(
            src_ref=tgt_ref.at[pl.ds(row, 1)], dst_ref=tgt_ref.at[pl.ds(slot, 1)], send_sem=row_send.at[k],
            recv_sem=row_recv.at[k], device_id=(row_at(k), col), device_id_type=MESH)

    def col_copy(k, slot):
        return pltpu.make_async_remote_copy(
            src_ref=src_ref.at[pl.ds(col, 1)], dst_ref=src_ref.at[pl.ds(slot, 1)], send_sem=col_send.at[k],
            recv_sem=col_recv.at[k], device_id=(row, moved(col, k, depth)), device_id_type=MESH)

    def om_copy(k, slot):
        return pltpu.make_async_remote_copy(
            src_ref=omegas_ref.at[pl.ds(col, 1)], dst_ref=omegas_ref.at[pl.ds(slot, 1)], send_sem=om_send.at[k],
            recv_sem=om_recv.at[k], device_id=(row, moved(col, k, depth)), device_id_type=MESH)

    def om_relay(k, slot):
        return pltpu.make_async_remote_copy(
            src_ref=omegas_ref.at[pl.ds(slot, 1)], dst_ref=omegas_ref.at[pl.ds(slot, 1)],
            send_sem=om_send.at[depth + k], recv_sem=om_recv.at[depth + k],
            device_id=(row, moved(col, depth, depth)), device_id_type=MESH)

    def hand_on(ks):
        for k in ks:
            om_copy(k, moved_back(col, k, depth)).wait_recv()
            om_relay(k, moved_back(col, k, depth)).start()

    near = sorted(range(1, depth), key=lambda k: min(k, depth - k))
    for k in deep[:cols // 2]:
        col_copy(k, col).start()
    for k in deep[cols // 2:]:
        col_copy(k, col).start()
    for k in wide:
        row_copy(k, row).start()
    om_relay(0, col).start()
    for k in near:
        om_copy(k, col).start()
    for k in wide:
        row_copy(k, row_back(k)).wait()
    prepare_targets(tgt_ref, tgt_base, tgt_feat, tgt_centre)
    for k in deep:
        col_copy(k, moved_back(col, k, depth)).wait()
    prepare_sources(src_ref, src_base, src_scale, src_feat, src_centre)
    table.wait()
    cut = len(near) // 2 + 1
    hand_on(near[:cut])

    def turned_step(i, carry):
        turned_group(i * GROUP, cols, meta_ref, tgt_base, src_feat, src_centre, turned_ref)

        @pl.when(i == 0)
        def _():
            hand_on(near[cut:-1])

        @pl.when(i == 1)
        def _():
            hand_on(near[-1:])

        return carry

    lax.fori_loop(0, groups, turned_step, 0)
    for k in near:
        om_copy(k, col).wait_send()
    for k in [0] + near:
        om_relay(k, col).wait_send()
        om_relay(k, col).wait_recv()

    def pair_copy(h, q):
        block = pl.ds(q * ring, ring)
        return pltpu.make_async_remote_copy(
            src_ref=stage_ref.at[h, block], dst_ref=pair_ref.at[h, block], send_sem=pair_send.at[h, q],
            recv_sem=pair_recv.at[h, q], device_id=(partner, col), device_id_type=MESH)

    def far_copy(h, k):
        return pltpu.make_async_remote_copy(
            src_ref=sum_ref.at[h, k], dst_ref=far_ref.at[h, k], send_sem=far_send.at[h, k],
            recv_sem=far_recv.at[h, k], device_id=(moved(chip, k, ring) * 2 + core, col), device_id_type=MESH)

    def swap(h):
        for q in (1, 0):
            for k in range(q * ring, (q + 1) * ring):
                stage_ref[h, k] = running_ref[h, meta_ref[2, 2 * moved(chip, k, ring) + 1 - core]]
            pair_copy(h, q).start()
        for k in range(chips):
            sum_ref[h, k] = running_ref[h, meta_ref[2, 2 * moved(chip, k, ring) + core]]

    def send_sums(h):
        for q in (1, 0):
            pair_copy(h, q).wait_recv()
            for k in [k for k in far if k // ring == q]:
                sum_ref[h, k] += pair_ref[h, k]
                far_copy(h, k).start()
        sum_ref[h, 0] += pair_ref[h, 0]

    def first_half(i, carry):
        sketch_group(i * GROUP, 0, cols, meta_ref, omegas_ref, turned_ref, running_ref)
        return carry

    def second_half(i, carry):
        @pl.when(i == groups - 1)
        def _():
            send_sums(0)

        sketch_group(i * GROUP, 1, cols, meta_ref, omegas_ref, turned_ref, running_ref)
        return carry

    lax.fori_loop(0, groups, first_half, 0)
    swap(0)
    lax.fori_loop(0, groups, second_half, 0)
    swap(1)

    def tile_step(i, carry):
        @pl.when(i == 1)
        def _():
            send_sums(1)

        tile_group(i * GROUP, cols, meta_ref, src_base, src_scale, tgt_feat, tgt_centre, tiles_ref)
        return carry

    lax.fori_loop(0, groups, tile_step, 0)

    totals, gram, energy = [], None, None
    for h in range(2):
        total = sum_ref[h, 0]
        for k in reversed(far):
            far_copy(h, k).wait_recv()
            total += far_ref[h, k]
        gram = gram_of(total) if h == 0 else gram + gram_of(total)
        energy = energy_of(total) if h == 0 else energy + energy_of(total)
        totals.append(total)

    part = rank // 2

    def out_copy(q, k, slot):
        block = all_ref.at[slot, pl.ds(q * part, part)]
        return pltpu.make_async_remote_copy(
            src_ref=block, dst_ref=block, send_sem=out_send.at[q, k], recv_sem=out_recv.at[q, k],
            device_id=(moved(chip, k, ring) * 2 + core, col), device_id_type=MESH)

    def relay_copy(q, k, slot):
        block = all_ref.at[slot, pl.ds(q * part, part)]
        return pltpu.make_async_remote_copy(
            src_ref=block, dst_ref=block, send_sem=relay_send.at[q, k], recv_sem=relay_recv.at[q, k],
            device_id=(partner, col), device_id_type=MESH)

    def send_part(q):
        block = pl.ds(q * part, part)
        all_ref[row, block] = basis_ref[0, block].astype(jnp.bfloat16)
        for k in far:
            out_copy(q, k, row).start()
        relay_copy(q, 0, row).start()

    factor(jnp.concatenate(totals, axis=1), gram, energy, basis_ref.at[0], lambda: send_part(0))
    send_part(1)
    for h in range(2):
        for k in far:
            far_copy(h, k).wait_send()
        for q in range(2):
            pair_copy(h, q).wait_send()
    for q in range(2):
        for k in reversed(far):
            slot = moved_back(chip, k, ring) * 2 + core
            out_copy(q, k, slot).wait_recv()
            relay_copy(q, k, slot).start()
    for q in range(2):
        for k in far:
            out_copy(q, k, row).wait_send()
        for k in [0] + far[::-1]:
            slot = moved_back(chip, k, ring) * 2 + core
            relay_copy(q, k, slot).wait_send()
            relay_copy(q, k, slot + 1 - 2 * core).wait_recv()


def sketch_and_factor(pairs, places, omega, rows, cols):
    slots = pairs.shape[1]
    rank, n = omega.shape[1], omega.shape[2]
    chips = rows // 2
    bf16, f32 = jnp.bfloat16, jnp.float32
    return pl.pallas_call(
        functools.partial(sketch_kernel, rows, cols),
        out_shape=[
            jax.ShapeDtypeStruct((slots, n, n), bf16),
            jax.ShapeDtypeStruct((1, rank, n), f32),
            jax.ShapeDtypeStruct((rows, rank, n), bf16),
            jax.ShapeDtypeStruct((8, slots), jnp.int32),
        ],
        in_specs=[pl.BlockSpec(memory_space=pltpu.HBM)] * 3,
        out_specs=[pl.BlockSpec(memory_space=VMEM)] * 4,
        scratch_shapes=[
            VMEM((2, slots), jnp.int32), SMEM((8, slots), jnp.int32),
            VMEM((rows,) + places.shape[1:], f32), VMEM((cols,) + places.shape[1:], f32),
            VMEM((cols, rank, n), bf16),
            VMEM((rows, 8, n), f32), VMEM((rows, n, 48), bf16), VMEM((rows, 8, n), f32),
            VMEM((cols, 8, n), f32), VMEM((cols, 8, n), f32), VMEM((cols, n, 48), bf16), VMEM((cols, 8, n), f32),
            VMEM((slots, n, n), bf16),
            VMEM((2, slots + 1, rank, n // 2), f32),
            VMEM((2, chips, rank, n // 2), f32), VMEM((2, chips, rank, n // 2), f32),
            VMEM((2, chips, rank, n // 2), f32), VMEM((2, chips, rank, n // 2), f32),
            DMA((5,)), DMA((rows,)), DMA((rows,)), DMA((cols,)), DMA((cols,)), DMA((cols,)), DMA((cols,)),
            DMA((2, 2)), DMA((2, 2)), DMA((2, chips)), DMA((2, chips)),
            DMA((2, chips)), DMA((2, chips)), DMA((2, chips)), DMA((2, chips)),
        ],
        compiler_params=pltpu.CompilerParams(collective_id=0, has_side_effects=True,
                                             vmem_limit_bytes=36 << 20),
        name="sketch_and_factor",
    )(*(pltpu.with_memory_space_constraint(x, pltpu.HBM) for x in (pairs, places, omega)))


def project_kernel(cols, meta_ref, basis_all_ref, basis_ref, tiles_ref, out_hbm, bases_ref, out_ref, out_sem):
    slots, n = tiles_ref.shape[0], tiles_ref.shape[1]

    def out_copy(i):
        part = pl.ds(i * PIECE, PIECE)
        return pltpu.make_async_copy(out_ref.at[part], out_hbm.at[part], out_sem.at[i])

    def step(i, carry):
        for g in range(LONG):
            p = i * LONG + g
            live = meta_ref[3, p].astype(jnp.float32)
            result = jnp.dot(basis_all_ref[meta_ref[0, p] // cols], tiles_ref[p],
                             preferred_element_type=jnp.float32)
            out_ref[p] = (result * live).astype(jnp.bfloat16)
            if (g + 1) % PIECE == 0:
                out_copy(i * (LONG // PIECE) + g // PIECE).start()
        return carry

    def finish(i, carry):
        out_copy(i).wait()
        return carry

    lax.fori_loop(0, slots // LONG, step, 0)
    bases_ref[...] = basis_ref[...] * math.sqrt(n)
    lax.fori_loop(0, slots // PIECE, finish, 0)


def project(meta, tiles, basis, basis_all, cols):
    slots = tiles.shape[0]
    rank, n = basis_all.shape[1], basis_all.shape[2]
    return pl.pallas_call(
        functools.partial(project_kernel, cols),
        out_shape=[
            jax.ShapeDtypeStruct((slots, rank, n), jnp.bfloat16),
            jax.ShapeDtypeStruct(basis.shape, basis.dtype),
        ],
        in_specs=[pl.BlockSpec(memory_space=SMEM)] + [pl.BlockSpec(memory_space=VMEM)] * 3,
        out_specs=[pl.BlockSpec(memory_space=pl.ANY), pl.BlockSpec(memory_space=VMEM)],
        scratch_shapes=[VMEM((slots, rank, n), jnp.bfloat16), DMA((slots // PIECE,))],
        compiler_params=pltpu.CompilerParams(vmem_limit_bytes=12 << 20),
        name="project",
    )(meta, basis_all, basis, tiles)


def body(places, omega, pairs):
    rows, cols = lax.axis_size("row"), lax.axis_size("col")
    pairs = pairs.T
    tiles, basis, basis_all, meta = sketch_and_factor(pairs, places, omega, rows, cols)
    coeffs, bases = project(meta, tiles, basis, basis_all, cols)
    return (bases, coeffs)


def solution(mesh):
    in_specs = (
        P(("row", "col"), None, None),
        P(("row", "col"), None, None),
        P(("row", "col"), None),
    )
    out_specs = (P(("row", "col"), None, None), P(("row", "col"), None, None))
    return jax.shard_map(body, mesh=mesh, in_specs=in_specs, out_specs=out_specs, check_vma=False)
```

```python
import functools
import math

import jax
import jax.numpy as jnp
from jax import lax
from jax.experimental import pallas as pl
from jax.experimental.pallas import tpu as pltpu
from jax.sharding import PartitionSpec as P

soft_sq = 0.09
ridge = 0.05
MESH = pl.DeviceIdType.MESH
VMEM = pltpu.VMEM
SMEM = pltpu.SMEM
DMA = pltpu.SemaphoreType.DMA
GROUP = 32
LONG = 64
PIECE = 16
NT = (((1,), (1,)), ((), ()))


def slot_table(cols, pairs_ref, meta_ref):
    slots = pairs_ref.shape[1]
    tgt_row = jnp.broadcast_to(pairs_ref[0:1], (slots, slots))
    src_row = jnp.broadcast_to(pairs_ref[1:2], (8, slots))
    tgt = tgt_row.T
    at_col = lax.broadcasted_iota(jnp.int32, (slots, slots), 0)
    at_row = lax.broadcasted_iota(jnp.int32, (slots, slots), 1)
    same = (tgt == tgt_row) & (tgt >= 0) & (at_col < at_row)
    last_of = (tgt >= 0) & (tgt // cols == at_row)

    def top(mask):
        best = jnp.where(mask, at_col, -1)
        rows = slots
        while rows > 8:
            rows //= 2
            best = jnp.maximum(best[:rows], best[rows:])
        for shift in (4, 2, 1):
            best = jnp.maximum(best, pltpu.roll(best, shift, 0))
        return jnp.where(best < 0, slots, best)

    live = tgt_row[0:8] >= 0
    code = jnp.where(live, tgt_row[0:8] // cols * cols + src_row % cols, 0)
    row = lax.broadcasted_iota(jnp.int32, (8, slots), 0)
    meta = jnp.where(row == 0, code, jnp.where(row == 1, top(same), top(last_of)))
    meta_ref[...] = jnp.where(row == 3, live.astype(jnp.int32), meta)


def split(x):
    hi = x.astype(jnp.bfloat16).astype(jnp.float32)
    rest = x - hi
    mid = rest.astype(jnp.bfloat16).astype(jnp.float32)
    return hi, mid, rest - mid


def coords_of(spots):
    return jnp.concatenate([spots[0:3], jnp.zeros((5, spots.shape[1]), jnp.float32)], axis=0)


def streamed(base, scale, row8):
    centre = jnp.sum(base, axis=1, keepdims=True) * (1.0 / base.shape[1])
    moved = base - centre
    norm = jnp.sum(moved * moved, axis=0, keepdims=True) + soft_sq
    feats = scale * jnp.where(row8 == 3, norm, jnp.where(row8 == 4, 1.0, -2.0 * moved))
    hi, mid, low = split(feats)
    stack = jnp.concatenate([hi, mid, low, hi, mid, hi], axis=0)
    return stack.T.astype(jnp.bfloat16), jnp.broadcast_to(centre, base.shape)


def held(base, scale, centre, row8):
    moved = base - centre
    norm = jnp.sum(moved * moved, axis=0, keepdims=True)
    feats = scale * jnp.where(row8 == 3, 1.0, jnp.where(row8 == 4, norm, moved))
    hi, mid, low = split(feats)
    return jnp.concatenate([hi, hi, hi, mid, mid, low], axis=0).astype(jnp.bfloat16)


def prepare_targets(tgt_ref, base_ref, feat_ref, centre_ref):
    n = tgt_ref.shape[2]
    row8 = lax.broadcasted_iota(jnp.int32, (8, n), 0)

    def one(t, carry):
        base = coords_of(tgt_ref[t])
        base_ref[t] = base
        feat_ref[t], centre_ref[t] = streamed(base, 1.0, row8)
        return carry

    lax.fori_loop(0, tgt_ref.shape[0], one, 0, unroll=4)


def prepare_sources(src_ref, base_ref, scale_ref, feat_ref, centre_ref):
    n = src_ref.shape[2]
    row8 = lax.broadcasted_iota(jnp.int32, (8, n), 0)

    def one(s, carry):
        spots = src_ref[s]
        base = coords_of(spots)
        weight = spots[3:4]
        scale = jnp.broadcast_to(1.0 / (weight * weight), (8, n))
        base_ref[s], scale_ref[s] = base, scale
        feat_ref[s], centre_ref[s] = streamed(base, scale, row8)
        return carry

    lax.fori_loop(0, src_ref.shape[0], one, 0, unroll=4)


def turned_group(first, cols, meta_ref, tgt_base, src_feat, src_centre, turned_ref):
    n = src_feat.shape[1]
    row8 = lax.broadcasted_iota(jnp.int32, (8, n), 0)
    for g in range(GROUP):
        code = meta_ref[0, first + g]
        t, s = code // cols, code % cols
        target = held(tgt_base[t], 1.0, src_centre[s], row8)
        dist = jnp.dot(src_feat[s], target, preferred_element_type=jnp.float32)
        turned_ref[first + g] = lax.rsqrt(dist).astype(jnp.bfloat16)


def tile_group(first, cols, meta_ref, src_base, src_scale, tgt_feat, tgt_centre, tiles_ref):
    n = tgt_feat.shape[1]
    row8 = lax.broadcasted_iota(jnp.int32, (8, n), 0)
    for g in range(GROUP):
        code = meta_ref[0, first + g]
        t, s = code // cols, code % cols
        source = held(src_base[s], src_scale[s], tgt_centre[t], row8)
        dist = jnp.dot(tgt_feat[t], source, preferred_element_type=jnp.float32)
        tiles_ref[first + g] = lax.rsqrt(dist).astype(jnp.bfloat16)


def sketch_group(first, h, cols, meta_ref, omegas_ref, turned_ref, running_ref):
    half = running_ref.shape[3]
    parts = []
    for g in range(LONG):
        s = meta_ref[0, first + g] % cols
        live = meta_ref[3, first + g].astype(jnp.float32)
        part = jnp.dot(omegas_ref[s], turned_ref[first + g, :, h * half:(h + 1) * half],
                       preferred_element_type=jnp.float32)
        parts.append(part * live)
    for g in range(LONG):
        running_ref[h, first + g] = running_ref[h, meta_ref[1, first + g]] + parts[g]


def gram_of(sketch):
    return lax.dot_general(sketch, sketch, NT, precision=lax.Precision.HIGHEST,
                           preferred_element_type=jnp.float32)


def energy_of(sketch):
    return jnp.sum(jnp.sum(sketch * sketch, axis=0, keepdims=True), axis=1, keepdims=True)


def factor(sketch, gram, energy, out, at_half):
    rank, width = sketch.shape
    shift = ridge * energy / rank
    eye = (lax.broadcasted_iota(jnp.int32, (rank, rank), 0)
           == lax.broadcasted_iota(jnp.int32, (rank, rank), 1))
    mat = gram + jnp.where(eye, shift, 0.0)

    def wide(x):
        return jnp.concatenate([x] * (width // 128), axis=1)

    for b in range(0, rank, 8):
        rows = rank - b
        row_at = lax.broadcasted_iota(jnp.int32, (rows, 1), 0)
        columns = [jnp.broadcast_to(mat[:, b + j:b + j + 1], (rows, 128)) for j in range(8)]
        for k in range(8):
            inv = lax.rsqrt(columns[k][k:k + 1])
            mult = jnp.where(row_at > k, columns[k] * inv, 0.0)
            mat_row = mat[k:k + 1] * inv[:, :rank]
            sketch_row = sketch[k:k + 1] * wide(inv)
            out[b + k:b + k + 1, :] = sketch_row
            for j in range(k + 1, 8):
                columns[j] = columns[j] - mult * (columns[j][k:k + 1] * inv)
            mat = mat - mult[:, :rank] * mat_row
            sketch = sketch - wide(mult) * sketch_row
        mat, sketch = mat[8:], sketch[8:]
        if 2 * (b + 8) == rank:
            at_half()


def sketch_kernel(rows, cols, pairs_hbm, places_ref, omega_ref, tiles_ref, basis_ref, all_ref, table_ref,
                  pairs_ref, meta_ref, tgt_ref, src_ref, omegas_ref, tgt_base, tgt_feat, tgt_centre,
                  src_base, src_scale, src_feat, src_centre, turned_ref, running_ref, stage_ref, pair_ref, sum_ref, far_ref,
                  own_sem, row_send, row_recv, col_send, col_recv, om_send, om_recv,
                  pair_send, pair_recv, far_send, far_recv, out_send, out_recv, relay_send, relay_recv):
    row, col = lax.axis_index("row"), lax.axis_index("col")
    core, chip, chips = lax.rem(row, 2), row // 2, rows // 2
    partner = row + 1 - 2 * core
    slots = tiles_ref.shape[0]
    groups = slots // GROUP
    rank, half = running_ref.shape[2], running_ref.shape[3]
    ring, depth = chips // 2, cols // 2

    def moved(at, k, size):
        return lax.rem(at // size + k // size, 2) * size + lax.rem(lax.rem(at, size) + k % size, size)

    def moved_back(at, k, size):
        return lax.rem(at // size + k // size, 2) * size + lax.rem(lax.rem(at, size) + size - k % size, size)

    far = sorted(range(1, chips), key=lambda k: -(k // ring + min(k % ring, ring - k % ring)))
    deep = sorted(range(1, cols), key=lambda k: -(2 * (k // depth) + min(k % depth, depth - k % depth)))
    wide = [2 * k + c for k in far + [0] for c in (0, 1) if 2 * k + c]

    def row_at(k):
        return moved(chip, k // 2, ring) * 2 + lax.rem(core + k % 2, 2)

    def row_back(k):
        return moved_back(chip, k // 2, ring) * 2 + lax.rem(core + k % 2, 2)

    slot_copy = pltpu.make_async_copy(pairs_hbm, pairs_ref, own_sem.at[4])
    slot_copy.start()
    barrier = pltpu.get_barrier_semaphore()
    for k in deep:
        pl.semaphore_signal(barrier, inc=1, device_id=(row, moved(col, k, depth)), device_id_type=MESH)
    for k in wide:
        pl.semaphore_signal(barrier, inc=1, device_id=(row_at(k), col), device_id_type=MESH)
    own = [
        pltpu.make_async_copy(places_ref, tgt_ref.at[pl.ds(row, 1)], own_sem.at[0]),
        pltpu.make_async_copy(places_ref, src_ref.at[pl.ds(col, 1)], own_sem.at[1]),
        pltpu.make_async_copy(omega_ref, omegas_ref.at[pl.ds(col, 1)], own_sem.at[2]),
    ]
    for c in own:
        c.start()
    slot_copy.wait()
    slot_table(cols, pairs_ref, table_ref)
    table = pltpu.make_async_copy(table_ref, meta_ref, own_sem.at[3])
    table.start()
    for h in range(2):
        running_ref[h, slots] = jnp.zeros((rank, half), jnp.float32)
    for c in own:
        c.wait()
    pl.semaphore_wait(barrier, rows + cols - 2)

    def row_copy(k, slot):
        return pltpu.make_async_remote_copy(
            src_ref=tgt_ref.at[pl.ds(row, 1)], dst_ref=tgt_ref.at[pl.ds(slot, 1)], send_sem=row_send.at[k],
            recv_sem=row_recv.at[k], device_id=(row_at(k), col), device_id_type=MESH)

    def col_copy(k, slot):
        return pltpu.make_async_remote_copy(
            src_ref=src_ref.at[pl.ds(col, 1)], dst_ref=src_ref.at[pl.ds(slot, 1)], send_sem=col_send.at[k],
            recv_sem=col_recv.at[k], device_id=(row, moved(col, k, depth)), device_id_type=MESH)

    def om_copy(k, slot):
        return pltpu.make_async_remote_copy(
            src_ref=omegas_ref.at[pl.ds(col, 1)], dst_ref=omegas_ref.at[pl.ds(slot, 1)], send_sem=om_send.at[k],
            recv_sem=om_recv.at[k], device_id=(row, moved(col, k, depth)), device_id_type=MESH)

    def om_relay(k, slot):
        return pltpu.make_async_remote_copy(
            src_ref=omegas_ref.at[pl.ds(slot, 1)], dst_ref=omegas_ref.at[pl.ds(slot, 1)],
            send_sem=om_send.at[depth + k], recv_sem=om_recv.at[depth + k],
            device_id=(row, moved(col, depth, depth)), device_id_type=MESH)

    def hand_on(ks):
        for k in ks:
            om_copy(k, moved_back(col, k, depth)).wait_recv()
            om_relay(k, moved_back(col, k, depth)).start()

    near = sorted(range(1, depth), key=lambda k: min(k, depth - k))
    for k in deep[:cols // 2]:
        col_copy(k, col).start()
    for k in deep[cols // 2:]:
        col_copy(k, col).start()
    for k in wide:
        row_copy(k, row).start()
    om_relay(0, col).start()
    for k in near:
        om_copy(k, col).start()
    for k in wide:
        row_copy(k, row_back(k)).wait()
    prepare_targets(tgt_ref, tgt_base, tgt_feat, tgt_centre)
    for k in deep:
        col_copy(k, moved_back(col, k, depth)).wait()
    prepare_sources(src_ref, src_base, src_scale, src_feat, src_centre)
    table.wait()
    cut = len(near) // 2 + 1
    hand_on(near[:cut])

    def turned_step(i, carry):
        turned_group(i * GROUP, cols, meta_ref, tgt_base, src_feat, src_centre, turned_ref)

        @pl.when(i == 0)
        def _():
            hand_on(near[cut:-1])

        @pl.when(i == 1)
        def _():
            hand_on(near[-1:])

        return carry

    lax.fori_loop(0, groups, turned_step, 0)
    for k in near:
        om_copy(k, col).wait_send()
    for k in [0] + near:
        om_relay(k, col).wait_send()
        om_relay(k, col).wait_recv()

    def pair_copy(h, q):
        block = pl.ds(q * ring, ring)
        return pltpu.make_async_remote_copy(
            src_ref=stage_ref.at[h, block], dst_ref=pair_ref.at[h, block], send_sem=pair_send.at[h, q],
            recv_sem=pair_recv.at[h, q], device_id=(partner, col), device_id_type=MESH)

    def far_copy(h, k):
        return pltpu.make_async_remote_copy(
            src_ref=sum_ref.at[h, k], dst_ref=far_ref.at[h, k], send_sem=far_send.at[h, k],
            recv_sem=far_recv.at[h, k], device_id=(moved(chip, k, ring) * 2 + core, col), device_id_type=MESH)

    def swap(h):
        for q in (1, 0):
            for k in range(q * ring, (q + 1) * ring):
                stage_ref[h, k] = running_ref[h, meta_ref[2, 2 * moved(chip, k, ring) + 1 - core]]
            pair_copy(h, q).start()
        for k in range(chips):
            sum_ref[h, k] = running_ref[h, meta_ref[2, 2 * moved(chip, k, ring) + core]]

    def send_sums(h):
        for q in (1, 0):
            pair_copy(h, q).wait_recv()
            for k in [k for k in far if k // ring == q]:
                sum_ref[h, k] += pair_ref[h, k]
                far_copy(h, k).start()
        sum_ref[h, 0] += pair_ref[h, 0]

    def first_half(i, carry):
        sketch_group(i * LONG, 0, cols, meta_ref, omegas_ref, turned_ref, running_ref)
        return carry

    def second_half(i, carry):
        @pl.when(i == slots // LONG - 1)
        def _():
            send_sums(0)

        sketch_group(i * LONG, 1, cols, meta_ref, omegas_ref, turned_ref, running_ref)
        return carry

    lax.fori_loop(0, slots // LONG, first_half, 0)
    swap(0)
    lax.fori_loop(0, slots // LONG, second_half, 0)
    swap(1)

    def tile_step(i, carry):
        @pl.when(i == 1)
        def _():
            send_sums(1)

        tile_group(i * GROUP, cols, meta_ref, src_base, src_scale, tgt_feat, tgt_centre, tiles_ref)
        return carry

    lax.fori_loop(0, groups, tile_step, 0)

    totals, gram, energy = [], None, None
    for h in range(2):
        total = sum_ref[h, 0]
        for k in reversed(far):
            far_copy(h, k).wait_recv()
            total += far_ref[h, k]
        gram = gram_of(total) if h == 0 else gram + gram_of(total)
        energy = energy_of(total) if h == 0 else energy + energy_of(total)
        totals.append(total)

    part = rank // 2

    def out_copy(q, k, slot):
        block = all_ref.at[slot, pl.ds(q * part, part)]
        return pltpu.make_async_remote_copy(
            src_ref=block, dst_ref=block, send_sem=out_send.at[q, k], recv_sem=out_recv.at[q, k],
            device_id=(moved(chip, k, ring) * 2 + core, col), device_id_type=MESH)

    def relay_copy(q, k, slot):
        block = all_ref.at[slot, pl.ds(q * part, part)]
        return pltpu.make_async_remote_copy(
            src_ref=block, dst_ref=block, send_sem=relay_send.at[q, k], recv_sem=relay_recv.at[q, k],
            device_id=(partner, col), device_id_type=MESH)

    def send_part(q):
        block = pl.ds(q * part, part)
        all_ref[row, block] = basis_ref[0, block].astype(jnp.bfloat16)
        for k in far:
            out_copy(q, k, row).start()
        relay_copy(q, 0, row).start()

    factor(jnp.concatenate(totals, axis=1), gram, energy, basis_ref.at[0], lambda: send_part(0))
    send_part(1)
    for h in range(2):
        for k in far:
            far_copy(h, k).wait_send()
        for q in range(2):
            pair_copy(h, q).wait_send()
    for q in range(2):
        for k in reversed(far):
            slot = moved_back(chip, k, ring) * 2 + core
            out_copy(q, k, slot).wait_recv()
            relay_copy(q, k, slot).start()
    for q in range(2):
        for k in far:
            out_copy(q, k, row).wait_send()
        for k in [0] + far[::-1]:
            slot = moved_back(chip, k, ring) * 2 + core
            relay_copy(q, k, slot).wait_send()
            relay_copy(q, k, slot + 1 - 2 * core).wait_recv()


def sketch_and_factor(pairs, places, omega, rows, cols):
    slots = pairs.shape[1]
    rank, n = omega.shape[1], omega.shape[2]
    chips = rows // 2
    bf16, f32 = jnp.bfloat16, jnp.float32
    return pl.pallas_call(
        functools.partial(sketch_kernel, rows, cols),
        out_shape=[
            jax.ShapeDtypeStruct((slots, n, n), bf16),
            jax.ShapeDtypeStruct((1, rank, n), f32),
            jax.ShapeDtypeStruct((rows, rank, n), bf16),
            jax.ShapeDtypeStruct((8, slots), jnp.int32),
        ],
        in_specs=[pl.BlockSpec(memory_space=pltpu.HBM)] * 3,
        out_specs=[pl.BlockSpec(memory_space=VMEM)] * 4,
        scratch_shapes=[
            VMEM((2, slots), jnp.int32), SMEM((8, slots), jnp.int32),
            VMEM((rows,) + places.shape[1:], f32), VMEM((cols,) + places.shape[1:], f32),
            VMEM((cols, rank, n), bf16),
            VMEM((rows, 8, n), f32), VMEM((rows, n, 48), bf16), VMEM((rows, 8, n), f32),
            VMEM((cols, 8, n), f32), VMEM((cols, 8, n), f32), VMEM((cols, n, 48), bf16), VMEM((cols, 8, n), f32),
            VMEM((slots, n, n), bf16),
            VMEM((2, slots + 1, rank, n // 2), f32),
            VMEM((2, chips, rank, n // 2), f32), VMEM((2, chips, rank, n // 2), f32),
            VMEM((2, chips, rank, n // 2), f32), VMEM((2, chips, rank, n // 2), f32),
            DMA((5,)), DMA((rows,)), DMA((rows,)), DMA((cols,)), DMA((cols,)), DMA((cols,)), DMA((cols,)),
            DMA((2, 2)), DMA((2, 2)), DMA((2, chips)), DMA((2, chips)),
            DMA((2, chips)), DMA((2, chips)), DMA((2, chips)), DMA((2, chips)),
        ],
        compiler_params=pltpu.CompilerParams(collective_id=0, has_side_effects=True,
                                             vmem_limit_bytes=36 << 20),
        name="sketch_and_factor",
    )(*(pltpu.with_memory_space_constraint(x, pltpu.HBM) for x in (pairs, places, omega)))


def project_kernel(cols, meta_ref, basis_all_ref, basis_ref, tiles_ref, out_hbm, bases_ref, out_ref, out_sem):
    slots, n = tiles_ref.shape[0], tiles_ref.shape[1]

    def out_copy(i):
        part = pl.ds(i * PIECE, PIECE)
        return pltpu.make_async_copy(out_ref.at[part], out_hbm.at[part], out_sem.at[i])

    def step(i, carry):
        for g in range(LONG):
            p = i * LONG + g
            live = meta_ref[3, p].astype(jnp.float32)
            result = jnp.dot(basis_all_ref[meta_ref[0, p] // cols], tiles_ref[p],
                             preferred_element_type=jnp.float32)
            out_ref[p] = (result * live).astype(jnp.bfloat16)
            if (g + 1) % PIECE == 0:
                out_copy(i * (LONG // PIECE) + g // PIECE).start()
        return carry

    def finish(i, carry):
        out_copy(i).wait()
        return carry

    lax.fori_loop(0, slots // LONG, step, 0)
    bases_ref[...] = basis_ref[...] * math.sqrt(n)
    lax.fori_loop(0, slots // PIECE, finish, 0)


def project(meta, tiles, basis, basis_all, cols):
    slots = tiles.shape[0]
    rank, n = basis_all.shape[1], basis_all.shape[2]
    return pl.pallas_call(
        functools.partial(project_kernel, cols),
        out_shape=[
            jax.ShapeDtypeStruct((slots, rank, n), jnp.bfloat16),
            jax.ShapeDtypeStruct(basis.shape, basis.dtype),
        ],
        in_specs=[pl.BlockSpec(memory_space=SMEM)] + [pl.BlockSpec(memory_space=VMEM)] * 3,
        out_specs=[pl.BlockSpec(memory_space=pl.ANY), pl.BlockSpec(memory_space=VMEM)],
        scratch_shapes=[VMEM((slots, rank, n), jnp.bfloat16), DMA((slots // PIECE,))],
        compiler_params=pltpu.CompilerParams(vmem_limit_bytes=12 << 20),
        name="project",
    )(meta, basis_all, basis, tiles)


def body(places, omega, pairs):
    rows, cols = lax.axis_size("row"), lax.axis_size("col")
    pairs = pairs.T
    tiles, basis, basis_all, meta = sketch_and_factor(pairs, places, omega, rows, cols)
    coeffs, bases = project(meta, tiles, basis, basis_all, cols)
    return (bases, coeffs)


def solution(mesh):
    in_specs = (
        P(("row", "col"), None, None),
        P(("row", "col"), None, None),
        P(("row", "col"), None),
    )
    out_specs = (P(("row", "col"), None, None), P(("row", "col"), None, None))
    return jax.shard_map(body, mesh=mesh, in_specs=in_specs, out_specs=out_specs, check_vma=False)
```
